256 devices in a mesh: frame: 16 (over z_hi, y), ref: 16 (over z_lo, x, core).
Axes of the slice: x: 4, y: 4, z: 8 (z_hi: 4, z_lo: 2; z = z_hi * 2 + z_lo), core: 2. Of those that a mesh axis runs over, the one named last changes fastest.
Arguments:
- latents: bfloat16 [16, 16, 256, 640], P('ref', 'frame'), may hold values from -6 to 6
- ref_hidden: bfloat16 [256, 640], P('ref'), may hold values from -6 to 6
- spatial_query: bfloat16 [640, 640], replicated, may hold values from -16 to 16
- spatial_key: bfloat16 [640, 640], replicated, may hold values from -1 to 1
- spatial_value: bfloat16 [640, 640], replicated, may hold values from -0.25 to 0.25
- spatial_out_w: bfloat16 [640, 640], replicated, may hold values from -0.25 to 0.25
- temporal_query: bfloat16 [640, 640], replicated, may hold values from -16 to 16
- temporal_key: bfloat16 [640, 640], replicated, may hold values from -1 to 1
- temporal_value: bfloat16 [640, 640], replicated, may hold values from -0.25 to 0.25
- temporal_out_w: bfloat16 [640, 640], replicated, may hold values from -0.25 to 0.25
Outputs:
- spatial_out: bfloat16 [16, 16, 256, 640], P('ref', 'frame')
- video_out: bfloat16 [16, 16, 256, 640], P('ref', 'frame')
The draws below stay inside these ranges and needn't reach their ends.
All inputs are finite; a program needn't handle non-finite values.
Results may differ from the reference program's by a relative error of at most 0.014.
Values may be sent and summed in bfloat16 or wider, within the bound.
A program may use at most 64 MiB of HBM per device.

```python
import math
import jax
import jax.numpy as jnp
from jax import lax

C = 640
HEADS = 8
TOKS = 256
CLIP = 16
CLIPS = 16


def drawn_base(key, tag):
    base_key = jax.random.fold_in(key, tag)
    normal_entries = jnp.clip(jax.random.normal(base_key, (C, C), jnp.float32), -5.0, 5.0)
    return normal_entries * (1.6 / math.sqrt(C))


def fresh_matrix(key):
    normal_entries = jnp.clip(jax.random.normal(key, (C, C), jnp.float32), -5.0, 5.0)
    return normal_entries * (1.6 / math.sqrt(C))


def draw_spatial_key(key, part):
    shared = drawn_base(key, 101)
    return shared.astype(jnp.bfloat16)


def draw_spatial_query(key, part):
    key = jax.random.fold_in(key, 4)
    return fresh_matrix(key).astype(jnp.bfloat16)


def draw_temporal_key(key, part):
    shared = drawn_base(key, 202)
    return shared.astype(jnp.bfloat16)


def draw_temporal_query(key, part):
    key = jax.random.fold_in(key, 6)
    return fresh_matrix(key).astype(jnp.bfloat16)


def steps_of(stream_key, extent, split, low, top_value):
    gain, own = 1.0, jax.random.fold_in(stream_key, 6)
    for axis_at, parts in split:
        draws = jnp.exp(jax.random.uniform(jax.random.fold_in(own, axis_at), (parts,), jnp.float32, low / len(split), top_value / len(split)))
        gain = gain * jnp.repeat(draws, extent[axis_at] // parts).reshape([-1 if axis == axis_at else 1 for axis in range(len(extent))])
    return gain


def noise(key, shape, deviation, bound, split=(), held_as=jnp.bfloat16):
    array = jax.random.normal(key, shape, jnp.float32) * deviation
    if len(split) > 0:
        array = steps_of(key, shape, split, -0.22, 0.18) * array
    return jnp.clip(array, min=-bound, max=bound).astype(held_as)


def setup_inputs(seed: int = 0) -> dict:
    streams_of = jax.random.split(jax.random.key(seed), 11)
    latents = noise(streams_of[0], (CLIPS, CLIP, TOKS, C), 1.0, 6.0, ((0, 16), (1, 16)))
    ref_hidden = noise(streams_of[1], (TOKS, C), 1.0, 6.0, ((0, 16),))
    spatial_query = draw_spatial_query(jax.random.fold_in(streams_of[10], 71), 0)
    spatial_key = draw_spatial_key(jax.random.fold_in(streams_of[10], 71), 0)
    spatial_value = noise(streams_of[4], (C, C), C ** -0.5, 0.25)
    spatial_out_w = noise(streams_of[5], (C, C), C ** -0.5, 0.25)
    temporal_query = draw_temporal_query(jax.random.fold_in(streams_of[10], 71), 0)
    temporal_key = draw_temporal_key(jax.random.fold_in(streams_of[10], 71), 0)
    temporal_value = noise(streams_of[8], (C, C), C ** -0.5, 0.25)
    temporal_out_w = noise(streams_of[9], (C, C), C ** -0.5, 0.25)
    return {"latents": latents, "ref_hidden": ref_hidden, "spatial_query": spatial_query, "spatial_key": spatial_key, "spatial_value": spatial_value, "spatial_out_w": spatial_out_w, "temporal_query": temporal_query, "temporal_key": temporal_key, "temporal_value": temporal_value, "temporal_out_w": temporal_out_w}


epsilon = 1e-05

def layer_norm(values_in):
    values_in = values_in.astype(jnp.float32)
    center = values_in - lax.optimization_barrier(jnp.mean(values_in, axis=-1, keepdims=True))
    spread = lax.optimization_barrier(jnp.mean(center * center, axis=-1, keepdims=True))
    return center * lax.rsqrt(spread + epsilon)

def sinusoid(count, width):
    position = jnp.arange(count, dtype=jnp.float32)[:, None]
    index_pair = jnp.arange(width // 2, dtype=jnp.float32)[None, :]
    angle = position * jnp.exp(index_pair * (-2.0 * math.log(10000.0) / width))
    return jnp.stack([jnp.sin(angle), jnp.cos(angle)], axis=-1).reshape(count, width)

def softmax_rows(scores):
    shifted = jnp.exp(scores - lax.optimization_barrier(jnp.max(scores, axis=-1, keepdims=True)))
    return (shifted / lax.optimization_barrier(jnp.sum(shifted, axis=-1, keepdims=True))).astype(jnp.bfloat16)

def attend_all(query_rows, key_rows, value_rows):
    row_count = query_rows.shape[0]
    head_dim = C // HEADS
    query_heads = query_rows.astype(jnp.float32).reshape(row_count, HEADS, head_dim)
    key_heads = key_rows.astype(jnp.float32).reshape(key_rows.shape[0], HEADS, head_dim)
    value_heads = value_rows.astype(jnp.float32).reshape(value_rows.shape[0], HEADS, head_dim)
    scores = jnp.einsum('rhd,khd->hrk', query_heads, key_heads) * (1.0 / math.sqrt(head_dim))
    weights = softmax_rows(scores)
    mixed = jnp.einsum('hrk,khd->rhd', weights.astype(jnp.float32), value_heads)
    return mixed.reshape(row_count, C).astype(jnp.bfloat16)

def project(rows, matrix):
    return jnp.dot(rows, matrix, preferred_element_type=jnp.float32).astype(jnp.bfloat16)

def reference(latents, ref_hidden, spatial_query, spatial_key, spatial_value, spatial_out_w, temporal_query, temporal_key, temporal_value, temporal_out_w):
    ref_norm = layer_norm(ref_hidden).astype(jnp.bfloat16)
    ref_keys = project(ref_norm, spatial_key)
    ref_values = project(ref_norm, spatial_value)

    def spatial(frame_rows):
        normed = layer_norm(frame_rows).astype(jnp.bfloat16)
        query_rows = project(normed, spatial_query)
        key_rows = jnp.concatenate([project(normed, spatial_key), ref_keys], axis=0)
        value_rows = jnp.concatenate([project(normed, spatial_value), ref_values], axis=0)
        attended = attend_all(query_rows, key_rows, value_rows)
        update = jnp.dot(attended, spatial_out_w, preferred_element_type=jnp.float32)
        return (frame_rows.astype(jnp.float32) + update).astype(jnp.bfloat16)
    spatial_out = lax.map(spatial, latents.reshape(CLIPS * CLIP, TOKS, C))
    position_code = sinusoid(CLIP, C)
    head_dim = C // HEADS

    def temporal(clip_rows):
        normed = (layer_norm(clip_rows) + position_code[:, None, :]).astype(jnp.bfloat16)
        flat = normed.reshape(CLIP * TOKS, C)
        query_heads = project(flat, temporal_query).astype(jnp.float32).reshape(CLIP, TOKS, HEADS, head_dim)
        key_heads = project(flat, temporal_key).astype(jnp.float32).reshape(CLIP, TOKS, HEADS, head_dim)
        value_heads = project(flat, temporal_value).astype(jnp.float32).reshape(CLIP, TOKS, HEADS, head_dim)
        scores = jnp.einsum('fthd,ethd->thfe', query_heads, key_heads) * (1.0 / math.sqrt(head_dim))
        weights = softmax_rows(scores)
        mixed = jnp.einsum('thfe,ethd->fthd', weights.astype(jnp.float32), value_heads)
        mixed = mixed.reshape(CLIP * TOKS, C).astype(jnp.bfloat16)
        update = jnp.dot(mixed, temporal_out_w, preferred_element_type=jnp.float32).reshape(CLIP, TOKS, C)
        return (clip_rows.astype(jnp.float32) + update).astype(jnp.bfloat16)
    video_out = lax.map(temporal, spatial_out.reshape(CLIPS, CLIP, TOKS, C))
    return (spatial_out.reshape(CLIPS, CLIP, TOKS, C), video_out)
```

```python
import functools
import math

import jax
import jax.numpy as jnp
import numpy as np
from jax import lax
from jax.experimental import pallas as pl
from jax.experimental.pallas import tpu as pltpu
from jax.sharding import PartitionSpec as P

MESH = pl.DeviceIdType.MESH
HEADS = 8
DIM = 80
WIDTH = 640
TOKENS = 256
FRAMES = 16
PIECES = 16
CHUNKS = 2
ROWS = TOKENS // CHUNKS
EACH = ROWS // FRAMES
EPSILON = 1e-05
SCALE = 1.0 / math.sqrt(DIM)
FACTOR = SCALE * math.log2(math.e)

FRAME_PEERS = sorted(
    [(a, b) for a in range(4) for b in range(4) if a or b],
    key=lambda o: -(2 * min(o[0], 4 - o[0]) + min(o[1], 4 - o[1])),
)
REF_PEERS = sorted(
    [(a, b, c) for a in range(2) for b in range(4) for c in range(2) if a or b or c],
    key=lambda o: -(2 * o[0] + 2 * min(o[1], 4 - o[1]) + o[2]),
)


def sinusoid(count, width):
    position = np.arange(count, dtype=np.float64)[:, None]
    pair = np.arange(width // 2, dtype=np.float64)[None, :]
    angle = position * np.exp(pair * (-2.0 * math.log(10000.0) / width))
    return np.stack([np.sin(angle), np.cos(angle)], axis=-1).reshape(count, width).astype(np.float32)


def layer_norm(rows):
    center = rows - jnp.mean(rows, axis=-1, keepdims=True)
    spread = jnp.mean(center * center, axis=-1, keepdims=True)
    return center * lax.rsqrt(spread + EPSILON)


def slab(head):
    low = head * DIM
    start = low // 128 * 128
    stop = -(-(low + DIM) // 128) * 128
    return start, stop - start, low - start


def head_lanes(head):
    start, wide, offset = slab(head)
    lane = lax.broadcasted_iota(jnp.int32, (1, wide), 1)
    return lane, (lane >= offset) & (lane < offset + DIM)


def ones_lane(head):
    start, wide, offset = slab(head)
    return 0 if offset > 0 else wide - 1


def masked_queries(rows, head):
    start, wide, _ = slab(head)
    _, inside = head_lanes(head)
    return jnp.where(inside, rows[:, start : start + wide], 0.0).astype(jnp.bfloat16)


def padded_values(rows, head):
    start, wide, _ = slab(head)
    lane, inside = head_lanes(head)
    filler = jnp.where(lane == ones_lane(head), 1.0, 0.0)
    return jnp.where(inside, rows[:, start : start + wide], filler).astype(jnp.bfloat16)


def attend(queries, keys_of, values_of, allowed=None):
    tiles = {}
    for head in range(HEADS):
        start, wide, offset = slab(head)
        scores = lax.dot_general(
            masked_queries(queries, head), keys_of(start, wide), (((1,), (1,)), ((), ())), preferred_element_type=jnp.float32
        )
        if allowed is not None:
            scores = jnp.where(allowed, scores, -1e30)
        top = jnp.max(scores, axis=-1, keepdims=True)
        weights = jnp.exp2((scores - top) * FACTOR).astype(jnp.bfloat16)
        mixed = jnp.dot(weights, values_of(head), preferred_element_type=jnp.float32)
        at = ones_lane(head)
        mixed = mixed * (1.0 / mixed[:, at : at + 1])
        lane, inside = head_lanes(head)
        for j in range(wide // 128):
            tile, cut = start // 128 + j, slice(j * 128, (j + 1) * 128)
            if tile in tiles:
                tiles[tile] = jnp.where(inside[:, cut], mixed[:, cut], tiles[tile])
            else:
                tiles[tile] = mixed[:, cut]
    return jnp.concatenate([tiles[t] for t in range(WIDTH // 128)], axis=1)


def project(rows, matrix):
    return jnp.dot(rows, matrix, preferred_element_type=jnp.float32)


def kernel(
    lat_hbm, ref_hbm, wq, wk, wv, wo, tq, tk, tv, to, pe_hbm,
    out_s, out_v,
    lat, ref_raw, ref_all, w, pe, queries, keys, values, own, got, back,
    load_sem, ref_send, ref_recv, go_send, go_recv, back_send, back_recv, out_sem,
):
    mine_f, mine_r = lax.axis_index("frame"), lax.axis_index("ref")
    zh, y = mine_f // 4, mine_f % 4
    zl, x, core = mine_r // 8, (mine_r // 2) % 4, mine_r % 2

    def frame_at(offset):
        return ((zh + offset[0]) % 4) * 4 + (y + offset[1]) % 4

    def ref_at(offset):
        return (((zl + offset[0]) % 2) * 4 + (x + offset[1]) % 4) * 2 + (core + offset[2]) % 2

    loads = [
        pltpu.make_async_copy(ref_hbm, ref_raw, load_sem.at[0]),
        pltpu.make_async_copy(lat_hbm, lat, load_sem.at[1]),
        pltpu.make_async_copy(pe_hbm, pe, load_sem.at[2]),
    ]
    weights = [
        pltpu.make_async_copy(matrix, w.at[i], load_sem.at[3 + i])
        for i, matrix in enumerate((wq, wk, wv, wo, tq, tk, tv, to))
    ]
    loads[0].start()
    loads[1].start()
    for copy in weights:
        copy.start()
    loads[2].start()

    barrier = pltpu.get_barrier_semaphore()
    for offset in FRAME_PEERS:
        pl.semaphore_signal(barrier, inc=1, device_id=(frame_at(offset), mine_r), device_id_type=MESH)
    for offset in REF_PEERS:
        pl.semaphore_signal(barrier, inc=1, device_id=(mine_f, ref_at(offset)), device_id_type=MESH)

    loads[0].wait()
    slot = pl.ds(pl.multiple_of(mine_r * PIECES, PIECES), PIECES)
    ref_all[slot, :] = layer_norm(ref_raw[...].astype(jnp.float32)).astype(jnp.bfloat16)
    pl.semaphore_wait(barrier, len(FRAME_PEERS) + len(REF_PEERS))
    ref_copies = []
    for k, offset in enumerate(REF_PEERS):
        copy = pltpu.make_async_remote_copy(
            src_ref=ref_all.at[slot, :], dst_ref=ref_all.at[slot, :],
            send_sem=ref_send.at[k], recv_sem=ref_recv.at[mine_r],
            device_id=(mine_f, ref_at(offset)), device_id_type=MESH,
        )
        copy.start()
        ref_copies.append(copy)

    loads[1].wait()
    normed = layer_norm(lat[...].astype(jnp.float32)).astype(jnp.bfloat16)
    weights[0].wait()
    queries[...] = project(normed, w[0]).astype(jnp.bfloat16)
    weights[1].wait()
    keys[0:TOKENS, :] = project(normed, w[1]).astype(jnp.bfloat16)
    weights[2].wait()
    own_values = project(normed, w[2]).astype(jnp.bfloat16)
    for head in range(HEADS):
        wide = slab(head)[1]
        values[head, 0:TOKENS, 0:wide] = padded_values(own_values, head)

    for k, offset in enumerate(REF_PEERS):
        source = ref_at(offset)
        there = pl.ds(pl.multiple_of(source * PIECES, PIECES), PIECES)
        pltpu.make_async_remote_copy(
            src_ref=ref_all.at[there, :], dst_ref=ref_all.at[there, :],
            send_sem=ref_send.at[k], recv_sem=ref_recv.at[source],
            device_id=(mine_f, source), device_id_type=MESH,
        ).wait_recv()
    reference = ref_all[...]
    keys[TOKENS : 2 * TOKENS, :] = project(reference, w[1]).astype(jnp.bfloat16)
    ref_values = project(reference, w[2]).astype(jnp.bfloat16)
    for head in range(HEADS):
        wide = slab(head)[1]
        values[head, TOKENS : 2 * TOKENS, 0:wide] = padded_values(ref_values, head)
    weights[3].wait()

    go_copies, out_copies = [], []
    for chunk in range(CHUNKS):
        rows = slice(chunk * ROWS, (chunk + 1) * ROWS)
        attended = attend(
            queries[rows, :],
            lambda start, wide: keys[:, start : start + wide],
            lambda head: values[head, :, 0 : slab(head)[1]],
        ).astype(jnp.bfloat16)
        result = lat[rows, :].astype(jnp.float32) + project(attended, w[3])
        own[chunk] = result.reshape(FRAMES, EACH, WIDTH).astype(jnp.bfloat16)
        for k, offset in enumerate(FRAME_PEERS):
            target = frame_at(offset)
            copy = pltpu.make_async_remote_copy(
                src_ref=own.at[chunk, target], dst_ref=got.at[chunk, mine_f],
                send_sem=go_send.at[chunk, k], recv_sem=go_recv.at[chunk, mine_f],
                device_id=(target, mine_r), device_id_type=MESH,
            )
            copy.start()
            go_copies.append(copy)
        got[chunk, pl.ds(mine_f, 1)] = own[chunk, pl.ds(mine_f, 1)]
        copy = pltpu.make_async_copy(
            own.at[chunk], out_s.at[pl.ds(chunk * FRAMES, FRAMES)], out_sem.at[chunk]
        )
        copy.start()
        out_copies.append(copy)

    loads[2].wait()
    for copy in weights[4:]:
        copy.wait()
    row = lax.broadcasted_iota(jnp.int32, (ROWS, ROWS), 0)
    column = lax.broadcasted_iota(jnp.int32, (ROWS, ROWS), 1)
    allowed = row % EACH == column % EACH
    back_copies = []
    for chunk in range(CHUNKS):
        for k, offset in enumerate(FRAME_PEERS):
            source = frame_at(offset)
            pltpu.make_async_remote_copy(
                src_ref=own.at[chunk, source], dst_ref=got.at[chunk, source],
                send_sem=go_send.at[chunk, k], recv_sem=go_recv.at[chunk, source],
                device_id=(source, mine_r), device_id_type=MESH,
            ).wait_recv()
        clip = got[chunk].astype(jnp.float32).reshape(ROWS, WIDTH)
        normed = (layer_norm(clip) + pe[...]).astype(jnp.bfloat16)
        time_queries = project(normed, w[4]).astype(jnp.bfloat16)
        time_keys = project(normed, w[5]).astype(jnp.bfloat16)
        time_values = project(normed, w[6]).astype(jnp.bfloat16)
        attended = attend(
            time_queries,
            lambda start, wide: time_keys[:, start : start + wide],
            lambda head: padded_values(time_values, head),
            allowed,
        ).astype(jnp.bfloat16)
        result = clip + project(attended, w[7])
        back[chunk] = result.reshape(FRAMES, EACH, WIDTH).astype(jnp.bfloat16)
        for k, offset in enumerate(FRAME_PEERS):
            target = frame_at(offset)
            copy = pltpu.make_async_remote_copy(
                src_ref=back.at[chunk, target], dst_ref=out_v.at[chunk * FRAMES + mine_f],
                send_sem=back_send.at[chunk, k], recv_sem=back_recv.at[chunk, mine_f],
                device_id=(target, mine_r), device_id_type=MESH,
            )
            copy.start()
            back_copies.append(copy)
        copy = pltpu.make_async_copy(
            back.at[chunk, mine_f], out_v.at[chunk * FRAMES + mine_f], out_sem.at[CHUNKS + chunk]
        )
        copy.start()
        out_copies.append(copy)

    for chunk in range(CHUNKS):
        for k, offset in enumerate(FRAME_PEERS):
            source = frame_at(offset)
            pltpu.make_async_remote_copy(
                src_ref=back.at[chunk, source], dst_ref=out_v.at[chunk * FRAMES + source],
                send_sem=back_send.at[chunk, k], recv_sem=back_recv.at[chunk, source],
                device_id=(source, mine_r), device_id_type=MESH,
            ).wait_recv()
    for copy in ref_copies + go_copies + back_copies:
        copy.wait_send()
    for copy in out_copies:
        copy.wait()


def body(latents, ref_hidden, *matrices):
    any_space = pl.BlockSpec(memory_space=pl.ANY)
    pe = jnp.asarray(np.repeat(sinusoid(FRAMES, WIDTH), EACH, axis=0))
    shape = jax.ShapeDtypeStruct((CHUNKS * FRAMES, EACH, WIDTH), jnp.bfloat16)
    spatial, video = pl.pallas_call(
        kernel,
        out_shape=(shape, shape),
        in_specs=[any_space] * 11,
        out_specs=(any_space, any_space),
        scratch_shapes=[
            pltpu.VMEM((TOKENS, WIDTH), jnp.bfloat16),
            pltpu.VMEM((PIECES, WIDTH), jnp.bfloat16),
            pltpu.VMEM((TOKENS, WIDTH), jnp.bfloat16),
            pltpu.VMEM((8, WIDTH, WIDTH), jnp.bfloat16),
            pltpu.VMEM((ROWS, WIDTH), jnp.float32),
            pltpu.VMEM((TOKENS, WIDTH), jnp.bfloat16),
            pltpu.VMEM((2 * TOKENS, WIDTH), jnp.bfloat16),
            pltpu.VMEM((HEADS, 2 * TOKENS, 256), jnp.bfloat16),
            pltpu.VMEM((CHUNKS, FRAMES, EACH, WIDTH), jnp.bfloat16),
            pltpu.VMEM((CHUNKS, FRAMES, EACH, WIDTH), jnp.bfloat16),
            pltpu.VMEM((CHUNKS, FRAMES, EACH, WIDTH), jnp.bfloat16),
            pltpu.SemaphoreType.DMA((11,)),
            pltpu.SemaphoreType.DMA((16,)),
            pltpu.SemaphoreType.DMA((16,)),
            pltpu.SemaphoreType.DMA((CHUNKS, 16)),
            pltpu.SemaphoreType.DMA((CHUNKS, 16)),
            pltpu.SemaphoreType.DMA((CHUNKS, 16)),
            pltpu.SemaphoreType.DMA((CHUNKS, 16)),
            pltpu.SemaphoreType.DMA((2 * CHUNKS,)),
        ],
        compiler_params=pltpu.CompilerParams(
            collective_id=0, has_side_effects=True, vmem_limit_bytes=48 * 2**20
        ),
        cost_estimate=pl.CostEstimate(flops=3_500_000_000, bytes_accessed=8_000_000, transcendentals=1_500_000),
    )(latents.reshape(TOKENS, WIDTH), ref_hidden, *matrices, pe)
    whole = (1, 1, TOKENS, WIDTH)
    return spatial.reshape(whole), video.reshape(whole)


def solution(mesh):
    split = P("ref", "frame", None, None)
    return jax.shard_map(
        body,
        mesh=mesh,
        in_specs=(split, P("ref", None)) + (P(),) * 8,
        out_specs=(split, split),
        check_vma=False,
    )
```

```python
import functools
import math

import jax
import jax.numpy as jnp
import numpy as np
from jax import lax
from jax.experimental import pallas as pl
from jax.experimental.pallas import tpu as pltpu
from jax.sharding import PartitionSpec as P

MESH = pl.DeviceIdType.MESH
HEADS = 8
DIM = 80
WIDTH = 640
TOKENS = 256
FRAMES = 16
PIECES = 16
CHUNKS = 2
ROWS = TOKENS // CHUNKS
EACH = ROWS // FRAMES
EPSILON = 1e-05
SCALE = 1.0 / math.sqrt(DIM)
FACTOR = SCALE * math.log2(math.e)

FRAME_PEERS = sorted(
    [(a, b) for a in range(4) for b in range(4) if a or b],
    key=lambda o: -(2 * min(o[0], 4 - o[0]) + min(o[1], 4 - o[1])),
)
REF_PEERS = sorted([(a, b) for a in range(2) for b in range(4) if a or b], key=lambda o: -(o[0] + min(o[1], 4 - o[1])))
NEAR = [(0, 1), (0, 2), (0, 3), (1, 0), (3, 0)]
ROW_PEERS = [(0, 1), (0, 2), (0, 3)]
COLUMN_PEERS = [(1, 0), (3, 0)]
HALF = TOKENS // 2


def sinusoid(count, width):
    position = np.arange(count, dtype=np.float64)[:, None]
    pair = np.arange(width // 2, dtype=np.float64)[None, :]
    angle = position * np.exp(pair * (-2.0 * math.log(10000.0) / width))
    return np.stack([np.sin(angle), np.cos(angle)], axis=-1).reshape(count, width).astype(np.float32)


def layer_norm(rows):
    center = rows - jnp.mean(rows, axis=-1, keepdims=True)
    spread = jnp.mean(center * center, axis=-1, keepdims=True)
    return center * lax.rsqrt(spread + EPSILON)


def slab(head):
    low = head * DIM
    start = low // 128 * 128
    stop = -(-(low + DIM) // 128) * 128
    return start, stop - start, low - start


def head_lanes(head):
    start, wide, offset = slab(head)
    lane = lax.broadcasted_iota(jnp.int32, (1, wide), 1)
    return lane, (lane >= offset) & (lane < offset + DIM)


def ones_lane(head):
    start, wide, offset = slab(head)
    return 0 if offset > 0 else wide - 1


def masked_queries(rows, head):
    start, wide, _ = slab(head)
    _, inside = head_lanes(head)
    return jnp.where(inside, rows[:, start : start + wide], 0.0).astype(jnp.bfloat16)


def padded_values(rows, head):
    start, wide, _ = slab(head)
    lane, inside = head_lanes(head)
    filler = jnp.where(lane == ones_lane(head), 1.0, 0.0)
    return jnp.where(inside, rows[:, start : start + wide], filler).astype(jnp.bfloat16)


def part(queries, keys, values, head, above=None):
    scores = lax.dot_general(queries, keys, (((1,), (1,)), ((), ())), preferred_element_type=jnp.float32)
    top = jnp.max(scores, axis=-1, keepdims=True)
    if above is not None:
        top = jnp.maximum(top, above)
    weights = jnp.exp2((scores - top) * FACTOR).astype(jnp.bfloat16)
    return top, jnp.dot(weights, values, preferred_element_type=jnp.float32)


def place(tiles, mixed, head):
    start, wide, _ = slab(head)
    _, inside = head_lanes(head)
    for j in range(wide // 128):
        tile, cut = start // 128 + j, slice(j * 128, (j + 1) * 128)
        if tile in tiles:
            tiles[tile] = jnp.where(inside[:, cut], mixed[:, cut], tiles[tile])
        else:
            tiles[tile] = mixed[:, cut]


def attend(queries, keys_of, values_of, allowed=None):
    tiles = {}
    for head in range(HEADS):
        start, wide, offset = slab(head)
        scores = lax.dot_general(
            masked_queries(queries, head), keys_of(start, wide), (((1,), (1,)), ((), ())), preferred_element_type=jnp.float32
        )
        if allowed is not None:
            scores = jnp.where(allowed, scores, -1e30)
        top = jnp.max(scores, axis=-1, keepdims=True)
        weights = jnp.exp2((scores - top) * FACTOR).astype(jnp.bfloat16)
        mixed = jnp.dot(weights, values_of(head), preferred_element_type=jnp.float32)
        at = ones_lane(head)
        mixed = mixed * (1.0 / mixed[:, at : at + 1])
        place(tiles, mixed, head)
    return jnp.concatenate([tiles[t] for t in range(WIDTH // 128)], axis=1)


def project(rows, matrix):
    return jnp.dot(rows, matrix, preferred_element_type=jnp.float32)


def kernel(
    lat_hbm, ref_hbm, wq, wk, wv, wo, tq, tk, tv, to, pe_hbm,
    out_s, out_v,
    lat, ref_raw, ref_all, w, pe, queries, keys, mixed_own, top_own, own, got, back,
    load_sem, ref_send, ref_recv, go_send, go_recv, back_send, back_recv, out_sem, row_sem, column_sem,
):
    mine_f, mine_r = lax.axis_index("frame"), lax.axis_index("ref")
    zh, y = mine_f // 4, mine_f % 4
    place_r, core = mine_r // 2, mine_r % 2
    zl, x = place_r // 4, place_r % 4

    def frame_at(offset):
        return ((zh + offset[0]) % 4) * 4 + (y + offset[1]) % 4

    def place_at(offset):
        return ((zl + offset[0]) % 2) * 4 + (x + offset[1]) % 4

    loads = [
        pltpu.make_async_copy(ref_hbm, ref_raw, load_sem.at[0]),
        pltpu.make_async_copy(lat_hbm, lat, load_sem.at[1]),
        pltpu.make_async_copy(pe_hbm, pe, load_sem.at[2]),
    ]
    weights = [
        pltpu.make_async_copy(matrix, w.at[i], load_sem.at[3 + i])
        for i, matrix in enumerate((wq, wk, wv, wo, tq, tk, tv, to))
    ]
    loads[0].start()
    barrier = pltpu.get_barrier_semaphore()
    sibling = (mine_f, place_r * 2 + 1 - core)
    greeted = [(mine_f, place_at(offset) * 2 + core) for offset in REF_PEERS]
    greeted += [sibling] + [(frame_at(offset), mine_r) for offset in NEAR]
    for device in greeted:
        pl.semaphore_signal(barrier, inc=1, device_id=device, device_id_type=MESH)
    loads[1].start()
    for copy in weights:
        copy.start()
    loads[2].start()

    loads[0].wait()
    slot = pl.ds(pl.multiple_of((core * 8 + place_r) * PIECES, PIECES), PIECES)
    ref_all[slot, :] = layer_norm(ref_raw[...].astype(jnp.float32)).astype(jnp.bfloat16)
    pl.semaphore_wait(barrier, len(greeted))
    ref_copies = []
    for k, offset in enumerate(REF_PEERS):
        copy = pltpu.make_async_remote_copy(
            src_ref=ref_all.at[slot, :], dst_ref=ref_all.at[slot, :],
            send_sem=ref_send.at[k], recv_sem=ref_recv.at[place_r],
            device_id=(mine_f, place_at(offset) * 2 + core), device_id_type=MESH,
        )
        copy.start()
        ref_copies.append(copy)
    for offset in COLUMN_PEERS:
        pl.semaphore_signal(column_sem, inc=1, device_id=(frame_at(offset), mine_r), device_id_type=MESH)

    loads[1].wait()
    normed = layer_norm(lat[...].astype(jnp.float32)).astype(jnp.bfloat16)
    weights[0].wait()
    queries[...] = project(normed, w[0]).astype(jnp.bfloat16)
    weights[1].wait()
    keys[...] = project(normed, w[1]).astype(jnp.bfloat16)
    weights[2].wait()
    own_values = project(normed, w[2]).astype(jnp.bfloat16)

    for head in range(HEADS):
        start, wide, _ = slab(head)
        cut = slice(start, start + wide)
        top, mixed = part(masked_queries(queries[...], head), keys[:, cut], padded_values(own_values, head), head)
        mixed_own[head, :, 0:wide] = mixed
        top_own[head] = jnp.broadcast_to(top, (TOKENS, 128))

    pl.semaphore_wait(column_sem, len(COLUMN_PEERS))
    for offset in ROW_PEERS:
        pl.semaphore_signal(row_sem, inc=1, device_id=(frame_at(offset), mine_r), device_id_type=MESH)

    for k, offset in enumerate(REF_PEERS):
        source = place_at(offset)
        there = pl.ds(pl.multiple_of((core * 8 + source) * PIECES, PIECES), PIECES)
        pltpu.make_async_remote_copy(
            src_ref=ref_all.at[there, :], dst_ref=ref_all.at[there, :],
            send_sem=ref_send.at[k], recv_sem=ref_recv.at[source],
            device_id=(mine_f, source * 2 + core), device_id_type=MESH,
        ).wait_recv()
    half = pl.ds(pl.multiple_of(core * HALF, HALF), HALF)
    copy = pltpu.make_async_remote_copy(
        src_ref=ref_all.at[half, :], dst_ref=ref_all.at[half, :],
        send_sem=ref_send.at[8], recv_sem=ref_recv.at[8],
        device_id=sibling, device_id_type=MESH,
    )
    copy.start()
    ref_copies.append(copy)
    weights[3].wait()
    copy.wait_recv()
    reference = ref_all[...]
    ref_keys = project(reference, w[1]).astype(jnp.bfloat16)
    ref_values = project(reference, w[2]).astype(jnp.bfloat16)

    tiles = {}
    for head in range(HEADS):
        start, wide, _ = slab(head)
        cut = slice(start, start + wide)
        before = top_own[head]
        top, mixed = part(
            masked_queries(queries[...], head), ref_keys[:, cut], padded_values(ref_values, head), head, before[:, 0:1]
        )
        kept = jnp.exp2((before - top) * FACTOR)
        mixed = mixed + mixed_own[head, :, 0:wide] * jnp.concatenate([kept] * (wide // 128), axis=1)
        at = ones_lane(head)
        place(tiles, mixed * (1.0 / mixed[:, at : at + 1]), head)
    attended = jnp.concatenate([tiles[t] for t in range(WIDTH // 128)], axis=1).astype(jnp.bfloat16)
    result = lat[...].astype(jnp.float32) + project(attended, w[3])
    own[...] = result.reshape(CHUNKS, FRAMES, EACH, WIDTH).astype(jnp.bfloat16)

    pl.semaphore_wait(row_sem, len(ROW_PEERS))
    go_copies, out_copies = [], []
    for chunk in range(CHUNKS):
        for k, offset in enumerate(FRAME_PEERS):
            target = frame_at(offset)
            copy = pltpu.make_async_remote_copy(
                src_ref=own.at[chunk, target], dst_ref=got.at[chunk, mine_f],
                send_sem=go_send.at[chunk, k], recv_sem=go_recv.at[chunk, mine_f],
                device_id=(target, mine_r), device_id_type=MESH,
            )
            copy.start()
            go_copies.append(copy)
    for chunk in range(CHUNKS):
        got[chunk, pl.ds(mine_f, 1)] = own[chunk, pl.ds(mine_f, 1)]
        copy = pltpu.make_async_copy(
            own.at[chunk], out_s.at[pl.ds(chunk * FRAMES, FRAMES)], out_sem.at[chunk]
        )
        copy.start()
        out_copies.append(copy)

    loads[2].wait()
    for copy in weights[4:]:
        copy.wait()
    row = lax.broadcasted_iota(jnp.int32, (ROWS, ROWS), 0)
    column = lax.broadcasted_iota(jnp.int32, (ROWS, ROWS), 1)
    allowed = row % EACH == column % EACH
    back_copies = []
    for chunk in range(CHUNKS):
        for k, offset in enumerate(FRAME_PEERS):
            source = frame_at(offset)
            pltpu.make_async_remote_copy(
                src_ref=own.at[chunk, source], dst_ref=got.at[chunk, source],
                send_sem=go_send.at[chunk, k], recv_sem=go_recv.at[chunk, source],
                device_id=(source, mine_r), device_id_type=MESH,
            ).wait_recv()
        clip = got[chunk].astype(jnp.float32).reshape(ROWS, WIDTH)
        normed = (layer_norm(clip) + pe[...]).astype(jnp.bfloat16)
        time_queries = project(normed, w[4]).astype(jnp.bfloat16)
        time_keys = project(normed, w[5]).astype(jnp.bfloat16)
        time_values = project(normed, w[6]).astype(jnp.bfloat16)
        attended = attend(
            time_queries,
            lambda start, wide: time_keys[:, start : start + wide],
            lambda head: padded_values(time_values, head),
            allowed,
        ).astype(jnp.bfloat16)
        result = clip + project(attended, w[7])
        back[chunk] = result.reshape(FRAMES, EACH, WIDTH).astype(jnp.bfloat16)
        for k, offset in enumerate(FRAME_PEERS):
            target = frame_at(offset)
            copy = pltpu.make_async_remote_copy(
                src_ref=back.at[chunk, target], dst_ref=out_v.at[chunk * FRAMES + mine_f],
                send_sem=back_send.at[chunk, k], recv_sem=back_recv.at[chunk, mine_f],
                device_id=(target, mine_r), device_id_type=MESH,
            )
            copy.start()
            back_copies.append(copy)
        copy = pltpu.make_async_copy(
            back.at[chunk, mine_f], out_v.at[chunk * FRAMES + mine_f], out_sem.at[CHUNKS + chunk]
        )
        copy.start()
        out_copies.append(copy)

    for chunk in range(CHUNKS):
        for k, offset in enumerate(FRAME_PEERS):
            source = frame_at(offset)
            pltpu.make_async_remote_copy(
                src_ref=back.at[chunk, source], dst_ref=out_v.at[chunk * FRAMES + source],
                send_sem=back_send.at[chunk, k], recv_sem=back_recv.at[chunk, source],
                device_id=(source, mine_r), device_id_type=MESH,
            ).wait_recv()
    for copy in ref_copies + go_copies + back_copies:
        copy.wait_send()
    for copy in out_copies:
        copy.wait()


def hand_over(spatial, video, out_s, out_v, sem):
    copies = [pltpu.make_async_copy(spatial, out_s, sem.at[0]), pltpu.make_async_copy(video, out_v, sem.at[1])]
    for copy in copies:
        copy.start()
    for copy in copies:
        copy.wait()


def body(latents, ref_hidden, *matrices):
    any_space = pl.BlockSpec(memory_space=pl.ANY)
    pe = jnp.asarray(np.repeat(sinusoid(FRAMES, WIDTH), EACH, axis=0))
    shape = jax.ShapeDtypeStruct((CHUNKS * FRAMES, EACH, WIDTH), jnp.bfloat16)
    spatial, video = pl.pallas_call(
        kernel,
        out_shape=(shape, shape),
        in_specs=[any_space] * 11,
        out_specs=(any_space, any_space),
        scratch_shapes=[
            pltpu.VMEM((TOKENS, WIDTH), jnp.bfloat16),
            pltpu.VMEM((PIECES, WIDTH), jnp.bfloat16),
            pltpu.VMEM((TOKENS, WIDTH), jnp.bfloat16),
            pltpu.VMEM((8, WIDTH, WIDTH), jnp.bfloat16),
            pltpu.VMEM((ROWS, WIDTH), jnp.float32),
            pltpu.VMEM((TOKENS, WIDTH), jnp.bfloat16),
            pltpu.VMEM((TOKENS, WIDTH), jnp.bfloat16),
            pltpu.VMEM((HEADS, TOKENS, 256), jnp.float32),
            pltpu.VMEM((HEADS, TOKENS, 128), jnp.float32),
            pltpu.VMEM((CHUNKS, FRAMES, EACH, WIDTH), jnp.bfloat16),
            pltpu.VMEM((CHUNKS, FRAMES, EACH, WIDTH), jnp.bfloat16),
            pltpu.VMEM((CHUNKS, FRAMES, EACH, WIDTH), jnp.bfloat16),
            pltpu.SemaphoreType.DMA((11,)),
            pltpu.SemaphoreType.DMA((16,)),
            pltpu.SemaphoreType.DMA((16,)),
            pltpu.SemaphoreType.DMA((CHUNKS, 16)),
            pltpu.SemaphoreType.DMA((CHUNKS, 16)),
            pltpu.SemaphoreType.DMA((CHUNKS, 16)),
            pltpu.SemaphoreType.DMA((CHUNKS, 16)),
            pltpu.SemaphoreType.DMA((2 * CHUNKS,)),
            pltpu.SemaphoreType.REGULAR,
            pltpu.SemaphoreType.REGULAR,
        ],
        compiler_params=pltpu.CompilerParams(
            collective_id=0, has_side_effects=True, vmem_limit_bytes=62 * 2**20
        ),
        cost_estimate=pl.CostEstimate(flops=3_500_000_000, bytes_accessed=8_000_000, transcendentals=1_500_000),
    )(latents.reshape(TOKENS, WIDTH), ref_hidden, *matrices, pe)
    spatial, video = pl.pallas_call(
        hand_over,
        out_shape=(shape, shape),
        in_specs=[any_space] * 2,
        out_specs=(any_space, any_space),
        scratch_shapes=[pltpu.SemaphoreType.DMA((2,))],
        compiler_params=pltpu.CompilerParams(vmem_limit_bytes=62 * 2**20),
    )(spatial, video)
    whole = (1, 1, TOKENS, WIDTH)
    return spatial.reshape(whole), video.reshape(whole)


def solution(mesh):
    split = P("ref", "frame", None, None)
    return jax.shard_map(
        body,
        mesh=mesh,
        in_specs=(split, P("ref", None)) + (P(),) * 8,
        out_specs=(split, split),
        check_vma=False,
    )
```

```python
import functools
import math

import jax
import jax.numpy as jnp
import numpy as np
from jax import lax
from jax.experimental import pallas as pl
from jax.experimental.pallas import tpu as pltpu
from jax.sharding import PartitionSpec as P

MESH = pl.DeviceIdType.MESH
HEADS = 8
DIM = 80
WIDTH = 640
TOKENS = 256
FRAMES = 16
PIECES = 16
CHUNKS = 2
ROWS = TOKENS // CHUNKS
EACH = ROWS // FRAMES
EPSILON = 1e-05
SCALE = 1.0 / math.sqrt(DIM)
FACTOR = SCALE * math.log2(math.e)

FRAME_PEERS = sorted(
    [(a, b) for a in range(4) for b in range(4) if a or b],
    key=lambda o: -(2 * min(o[0], 4 - o[0]) + min(o[1], 4 - o[1])),
)
REF_PEERS = sorted([(a, b) for a in range(2) for b in range(4) if a or b], key=lambda o: -(o[0] + min(o[1], 4 - o[1])))
NEAR = [(0, 1), (0, 2), (0, 3), (1, 0), (3, 0)]
ROW_PEERS = [(0, 1), (0, 2), (0, 3)]
COLUMN_PEERS = [(1, 0), (3, 0)]
HALF = TOKENS // 2


def sinusoid(count, width):
    position = np.arange(count, dtype=np.float64)[:, None]
    pair = np.arange(width // 2, dtype=np.float64)[None, :]
    angle = position * np.exp(pair * (-2.0 * math.log(10000.0) / width))
    return np.stack([np.sin(angle), np.cos(angle)], axis=-1).reshape(count, width).astype(np.float32)


def layer_norm(rows):
    center = rows - jnp.mean(rows, axis=-1, keepdims=True)
    spread = jnp.mean(center * center, axis=-1, keepdims=True)
    return center * lax.rsqrt(spread + EPSILON)


def slab(head):
    low = head * DIM
    start = low // 128 * 128
    stop = -(-(low + DIM) // 128) * 128
    return start, stop - start, low - start


def head_lanes(head):
    start, wide, offset = slab(head)
    lane = lax.broadcasted_iota(jnp.int32, (1, wide), 1)
    return lane, (lane >= offset) & (lane < offset + DIM)


def sum_lane(head):
    return head if head > 0 else 120


def masked_queries(rows, head):
    start, wide, _ = slab(head)
    _, inside = head_lanes(head)
    return jnp.where(inside, rows[:, start : start + wide], 0.0).astype(jnp.bfloat16)


def padded_values(rows, head):
    start, wide, _ = slab(head)
    lane, inside = head_lanes(head)
    filler = jnp.where(lane == sum_lane(head), 1.0, 0.0)
    return jnp.where(inside, rows[:, start : start + wide], filler).astype(jnp.bfloat16)


def attend(queries, keys, values, allowed=None):
    count = queries.shape[0]
    lane = lax.broadcasted_iota(jnp.int32, (1, 128), 1)
    tops, sums = jnp.zeros((count, 128), jnp.float32), jnp.ones((count, 128), jnp.float32)
    tiles = {}
    for head in range(HEADS):
        start, wide, _ = slab(head)
        _, inside = head_lanes(head)
        scores = lax.dot_general(
            masked_queries(queries, head), keys[:, start : start + wide],
            (((1,), (1,)), ((), ())), preferred_element_type=jnp.float32,
        )
        if allowed is not None:
            scores = jnp.where(allowed, scores, -1e30)
        top = jnp.max(scores, axis=-1, keepdims=True)
        weights = jnp.exp2((scores - top) * FACTOR).astype(jnp.bfloat16)
        mixed = jnp.dot(weights, padded_values(values, head), preferred_element_type=jnp.float32)
        tops = jnp.where(lane == sum_lane(head), top, tops)
        sums = jnp.where(lane == sum_lane(head), mixed[:, :128], sums)
        for j in range(wide // 128):
            tile, cut = start // 128 + j, slice(j * 128, (j + 1) * 128)
            if tile in tiles:
                tiles[tile] = jnp.where(inside[:, cut], mixed[:, cut], tiles[tile])
            else:
                tiles[tile] = mixed[:, cut]
    return jnp.concatenate([tiles[t] for t in range(WIDTH // 128)], axis=1), tops, sums


def head_columns():
    lane = lax.broadcasted_iota(jnp.int32, (256, WIDTH), 0) % 128
    head = lax.broadcasted_iota(jnp.int32, (256, WIDTH), 1) // DIM
    return jnp.where(lane == jnp.where(head == 0, sum_lane(0), head), 1.0, 0.0).astype(jnp.bfloat16)


def to_columns(factors, columns):
    high = factors.astype(jnp.bfloat16)
    low = (factors - high.astype(jnp.float32)).astype(jnp.bfloat16)
    return project(jnp.concatenate([high, low], axis=1), columns)


def project(rows, matrix):
    return jnp.dot(rows, matrix, preferred_element_type=jnp.float32)


def kernel(
    lat_hbm, ref_hbm, wq, wk, wv, wo, tq, tk, tv, to, pe_hbm,
    out_s, out_v,
    lat, ref_raw, ref_all, w, pe, queries, mixed_own, top_own, sum_own, columns, own, got, back,
    load_sem, ref_send, ref_recv, go_send, go_recv, back_send, back_recv, out_sem, row_sem, column_sem,
):
    mine_f, mine_r = lax.axis_index("frame"), lax.axis_index("ref")
    zh, y = mine_f // 4, mine_f % 4
    place_r, core = mine_r // 2, mine_r % 2
    zl, x = place_r // 4, place_r % 4

    def frame_at(offset):
        return ((zh + offset[0]) % 4) * 4 + (y + offset[1]) % 4

    def place_at(offset):
        return ((zl + offset[0]) % 2) * 4 + (x + offset[1]) % 4

    loads = [
        pltpu.make_async_copy(ref_hbm, ref_raw, load_sem.at[0]),
        pltpu.make_async_copy(lat_hbm, lat, load_sem.at[1]),
        pltpu.make_async_copy(pe_hbm, pe, load_sem.at[2]),
    ]
    weights = [
        pltpu.make_async_copy(matrix, w.at[i], load_sem.at[3 + i])
        for i, matrix in enumerate((wq, wk, wv, wo, tq, tk, tv, to))
    ]
    loads[0].start()
    barrier = pltpu.get_barrier_semaphore()
    sibling = (mine_f, place_r * 2 + 1 - core)
    greeted = [(mine_f, place_at(offset) * 2 + core) for offset in REF_PEERS]
    greeted += [sibling] + [(frame_at(offset), mine_r) for offset in NEAR]
    for device in greeted:
        pl.semaphore_signal(barrier, inc=1, device_id=device, device_id_type=MESH)
    loads[1].start()
    for copy in weights:
        copy.start()
    loads[2].start()

    loads[0].wait()
    slot = pl.ds(pl.multiple_of((core * 8 + place_r) * PIECES, PIECES), PIECES)
    ref_all[slot, :] = layer_norm(ref_raw[...].astype(jnp.float32)).astype(jnp.bfloat16)
    pl.semaphore_wait(barrier, len(greeted))
    ref_copies = []
    for k, offset in enumerate(REF_PEERS):
        copy = pltpu.make_async_remote_copy(
            src_ref=ref_all.at[slot, :], dst_ref=ref_all.at[slot, :],
            send_sem=ref_send.at[k], recv_sem=ref_recv.at[place_r],
            device_id=(mine_f, place_at(offset) * 2 + core), device_id_type=MESH,
        )
        copy.start()
        ref_copies.append(copy)
    for offset in COLUMN_PEERS:
        pl.semaphore_signal(column_sem, inc=1, device_id=(frame_at(offset), mine_r), device_id_type=MESH)

    loads[1].wait()
    normed = layer_norm(lat[...].astype(jnp.float32)).astype(jnp.bfloat16)
    weights[0].wait()
    queries[...] = project(normed, w[0]).astype(jnp.bfloat16)
    weights[1].wait()
    own_keys = project(normed, w[1]).astype(jnp.bfloat16)
    weights[2].wait()
    own_values = project(normed, w[2]).astype(jnp.bfloat16)

    mixed_own[...], top_own[...], sum_own[...] = attend(queries[...], own_keys, own_values)
    columns[...] = head_columns()

    pl.semaphore_wait(column_sem, len(COLUMN_PEERS))
    for offset in ROW_PEERS:
        pl.semaphore_signal(row_sem, inc=1, device_id=(frame_at(offset), mine_r), device_id_type=MESH)

    for k, offset in enumerate(REF_PEERS):
        source = place_at(offset)
        there = pl.ds(pl.multiple_of((core * 8 + source) * PIECES, PIECES), PIECES)
        pltpu.make_async_remote_copy(
            src_ref=ref_all.at[there, :], dst_ref=ref_all.at[there, :],
            send_sem=ref_send.at[k], recv_sem=ref_recv.at[source],
            device_id=(mine_f, source * 2 + core), device_id_type=MESH,
        ).wait_recv()
    half = pl.ds(pl.multiple_of(core * HALF, HALF), HALF)
    copy = pltpu.make_async_remote_copy(
        src_ref=ref_all.at[half, :], dst_ref=ref_all.at[half, :],
        send_sem=ref_send.at[8], recv_sem=ref_recv.at[8],
        device_id=sibling, device_id_type=MESH,
    )
    copy.start()
    ref_copies.append(copy)
    weights[3].wait()
    copy.wait_recv()
    reference = ref_all[...]
    ref_keys = project(reference, w[1]).astype(jnp.bfloat16)
    ref_values = project(reference, w[2]).astype(jnp.bfloat16)

    mixed, top_ref, sum_ref = attend(queries[...], ref_keys, ref_values)
    top = jnp.maximum(top_own[...], top_ref)
    kept_own, kept_ref = jnp.exp2((top_own[...] - top) * FACTOR), jnp.exp2((top_ref - top) * FACTOR)
    scale = 1.0 / (sum_own[...] * kept_own + sum_ref * kept_ref)
    attended = mixed_own[...] * to_columns(kept_own * scale, columns[...])
    attended = (attended + mixed * to_columns(kept_ref * scale, columns[...])).astype(jnp.bfloat16)
    result = lat[...].astype(jnp.float32) + project(attended, w[3])
    own[...] = result.reshape(CHUNKS, FRAMES, EACH, WIDTH).astype(jnp.bfloat16)

    pl.semaphore_wait(row_sem, len(ROW_PEERS))
    go_copies, out_copies = [], []
    for chunk in range(CHUNKS):
        for k, offset in enumerate(FRAME_PEERS):
            target = frame_at(offset)
            copy = pltpu.make_async_remote_copy(
                src_ref=own.at[chunk, target], dst_ref=got.at[chunk, mine_f],
                send_sem=go_send.at[chunk, k], recv_sem=go_recv.at[chunk, mine_f],
                device_id=(target, mine_r), device_id_type=MESH,
            )
            copy.start()
            go_copies.append(copy)
    for chunk in range(CHUNKS):
        got[chunk, pl.ds(mine_f, 1)] = own[chunk, pl.ds(mine_f, 1)]
        copy = pltpu.make_async_copy(
            own.at[chunk], out_s.at[pl.ds(chunk * FRAMES, FRAMES)], out_sem.at[chunk]
        )
        copy.start()
        out_copies.append(copy)

    loads[2].wait()
    for copy in weights[4:]:
        copy.wait()
    row = lax.broadcasted_iota(jnp.int32, (ROWS, ROWS), 0)
    column = lax.broadcasted_iota(jnp.int32, (ROWS, ROWS), 1)
    allowed = row % EACH == column % EACH
    back_copies = []
    for chunk in range(CHUNKS):
        for k, offset in enumerate(FRAME_PEERS):
            source = frame_at(offset)
            pltpu.make_async_remote_copy(
                src_ref=own.at[chunk, source], dst_ref=got.at[chunk, source],
                send_sem=go_send.at[chunk, k], recv_sem=go_recv.at[chunk, source],
                device_id=(source, mine_r), device_id_type=MESH,
            ).wait_recv()
        clip = got[chunk].astype(jnp.float32).reshape(ROWS, WIDTH)
        normed = (layer_norm(clip) + pe[...]).astype(jnp.bfloat16)
        time_queries = project(normed, w[4]).astype(jnp.bfloat16)
        time_keys = project(normed, w[5]).astype(jnp.bfloat16)
        time_values = project(normed, w[6]).astype(jnp.bfloat16)
        mixed, _, total = attend(time_queries, time_keys, time_values, allowed)
        attended = (mixed * to_columns(1.0 / total, columns[...])).astype(jnp.bfloat16)
        result = clip + project(attended, w[7])
        back[chunk] = result.reshape(FRAMES, EACH, WIDTH).astype(jnp.bfloat16)
        for k, offset in enumerate(FRAME_PEERS):
            target = frame_at(offset)
            copy = pltpu.make_async_remote_copy(
                src_ref=back.at[chunk, target], dst_ref=out_v.at[chunk * FRAMES + mine_f],
                send_sem=back_send.at[chunk, k], recv_sem=back_recv.at[chunk, mine_f],
                device_id=(target, mine_r), device_id_type=MESH,
            )
            copy.start()
            back_copies.append(copy)
        copy = pltpu.make_async_copy(
            back.at[chunk, mine_f], out_v.at[chunk * FRAMES + mine_f], out_sem.at[CHUNKS + chunk]
        )
        copy.start()
        out_copies.append(copy)

    for chunk in range(CHUNKS):
        for k, offset in enumerate(FRAME_PEERS):
            source = frame_at(offset)
            pltpu.make_async_remote_copy(
                src_ref=back.at[chunk, source], dst_ref=out_v.at[chunk * FRAMES + source],
                send_sem=back_send.at[chunk, k], recv_sem=back_recv.at[chunk, source],
                device_id=(source, mine_r), device_id_type=MESH,
            ).wait_recv()
    for copy in ref_copies + go_copies + back_copies:
        copy.wait_send()
    for copy in out_copies:
        copy.wait()


def hand_over(spatial, video, out_s, out_v, sem):
    copies = [pltpu.make_async_copy(spatial, out_s, sem.at[0]), pltpu.make_async_copy(video, out_v, sem.at[1])]
    for copy in copies:
        copy.start()
    for copy in copies:
        copy.wait()


def body(latents, ref_hidden, *matrices):
    any_space = pl.BlockSpec(memory_space=pl.ANY)
    pe = jnp.asarray(np.repeat(sinusoid(FRAMES, WIDTH), EACH, axis=0))
    shape = jax.ShapeDtypeStruct((CHUNKS * FRAMES, EACH, WIDTH), jnp.bfloat16)
    operands = (latents.reshape(TOKENS, WIDTH), ref_hidden, *matrices, pe)
    spatial, video = pl.pallas_call(
        kernel,
        out_shape=(shape, shape),
        in_specs=[any_space] * 11,
        out_specs=(any_space, any_space),
        scratch_shapes=[
            pltpu.VMEM((TOKENS, WIDTH), jnp.bfloat16),
            pltpu.VMEM((PIECES, WIDTH), jnp.bfloat16),
            pltpu.VMEM((TOKENS, WIDTH), jnp.bfloat16),
            pltpu.VMEM((8, WIDTH, WIDTH), jnp.bfloat16),
            pltpu.VMEM((ROWS, WIDTH), jnp.float32),
            pltpu.VMEM((TOKENS, WIDTH), jnp.bfloat16),
            pltpu.VMEM((TOKENS, WIDTH), jnp.float32),
            pltpu.VMEM((TOKENS, 128), jnp.float32),
            pltpu.VMEM((TOKENS, 128), jnp.float32),
            pltpu.VMEM((256, WIDTH), jnp.bfloat16),
            pltpu.VMEM((CHUNKS, FRAMES, EACH, WIDTH), jnp.bfloat16),
            pltpu.VMEM((CHUNKS, FRAMES, EACH, WIDTH), jnp.bfloat16),
            pltpu.VMEM((CHUNKS, FRAMES, EACH, WIDTH), jnp.bfloat16),
            pltpu.SemaphoreType.DMA((11,)),
            pltpu.SemaphoreType.DMA((16,)),
            pltpu.SemaphoreType.DMA((16,)),
            pltpu.SemaphoreType.DMA((CHUNKS, 16)),
            pltpu.SemaphoreType.DMA((CHUNKS, 16)),
            pltpu.SemaphoreType.DMA((CHUNKS, 16)),
            pltpu.SemaphoreType.DMA((CHUNKS, 16)),
            pltpu.SemaphoreType.DMA((2 * CHUNKS,)),
            pltpu.SemaphoreType.REGULAR,
            pltpu.SemaphoreType.REGULAR,
        ],
        compiler_params=pltpu.CompilerParams(
            collective_id=0, has_side_effects=True, vmem_limit_bytes=48 * 2**20
        ),
        cost_estimate=pl.CostEstimate(flops=3_500_000_000, bytes_accessed=8_000_000, transcendentals=1_500_000),
    )(*[pltpu.with_memory_space_constraint(a, pltpu.HBM) for a in operands])
    spatial, video = pl.pallas_call(
        hand_over,
        out_shape=(shape, shape),
        in_specs=[any_space] * 2,
        out_specs=(any_space, any_space),
        scratch_shapes=[pltpu.SemaphoreType.DMA((2,))],
        compiler_params=pltpu.CompilerParams(vmem_limit_bytes=48 * 2**20),
    )(spatial, video)
    whole = (1, 1, TOKENS, WIDTH)
    return spatial.reshape(whole), video.reshape(whole)


def solution(mesh):
    split = P("ref", "frame", None, None)
    return jax.shard_map(
        body,
        mesh=mesh,
        in_specs=(split, P("ref", None)) + (P(),) * 8,
        out_specs=(split, split),
        check_vma=False,
    )
```

```python
import functools
import math

import jax
import jax.numpy as jnp
import numpy as np
from jax import lax
from jax.experimental import pallas as pl
from jax.experimental.pallas import tpu as pltpu
from jax.sharding import PartitionSpec as P

MESH = pl.DeviceIdType.MESH
HEADS = 8
DIM = 80
WIDTH = 640
TOKENS = 256
FRAMES = 16
PIECES = 16
CHUNKS = 2
ROWS = TOKENS // CHUNKS
EACH = ROWS // FRAMES
EPSILON = 1e-05
SCALE = 1.0 / math.sqrt(DIM)
FACTOR = SCALE * math.log2(math.e)

FRAME_PEERS = sorted(
    [(a, b) for a in range(4) for b in range(4) if a or b],
    key=lambda o: -(2 * min(o[0], 4 - o[0]) + min(o[1], 4 - o[1])),
)
REF_PEERS = sorted([(a, b) for a in range(2) for b in range(4) if a or b], key=lambda o: -(o[0] + min(o[1], 4 - o[1])))
NEAR = [(0, 1), (0, 2), (0, 3), (1, 0), (3, 0)]
ROW_PEERS = [(0, 1), (0, 2), (0, 3)]
COLUMN_PEERS = [(1, 0), (3, 0)]
HALF = TOKENS // 2


def sinusoid(count, width):
    position = np.arange(count, dtype=np.float64)[:, None]
    pair = np.arange(width // 2, dtype=np.float64)[None, :]
    angle = position * np.exp(pair * (-2.0 * math.log(10000.0) / width))
    return np.stack([np.sin(angle), np.cos(angle)], axis=-1).reshape(count, width).astype(np.float32)


def layer_norm(rows):
    center = rows - jnp.mean(rows, axis=-1, keepdims=True)
    spread = jnp.mean(center * center, axis=-1, keepdims=True)
    return center * lax.rsqrt(spread + EPSILON)


GROUPS = (((0, 1, 2), 0), ((3,), 128), ((4,), 256), ((5, 6, 7), 384))


def sum_column(head):
    return 240 + head if head < 3 else {3: 128, 4: 256}.get(head, 384) + head


def attend(queries, keys, values, allowed=None):
    count = queries.shape[0]
    lane = lax.broadcasted_iota(jnp.int32, (1, 128), 1)
    column = lax.broadcasted_iota(jnp.int32, (1, 256), 1)
    tops, sums = jnp.zeros((count, 128), jnp.float32), jnp.ones((count, 128), jnp.float32)
    tiles = {}
    for heads, start in GROUPS:
        cut = slice(start, start + 256)
        stack = []
        for head in heads:
            inside = (column >= head * DIM - start) & (column < (head + 1) * DIM - start)
            stack.append(jnp.where(inside, queries[:, cut], 0.0).astype(jnp.bfloat16))
        scores = lax.dot_general(
            jnp.concatenate(stack, axis=0), keys[:, cut], (((1,), (1,)), ((), ())), preferred_element_type=jnp.float32
        )
        if allowed is not None:
            scores = jnp.where(jnp.concatenate([allowed] * len(heads), axis=0), scores, -1e30)
        top = jnp.max(scores, axis=-1, keepdims=True)
        weights = jnp.exp2((scores - top) * FACTOR).astype(jnp.bfloat16)
        window = values[:, cut]
        for head in heads:
            window = jnp.where(column == sum_column(head) - start, 1.0, window).astype(jnp.bfloat16)
        mixed = jnp.dot(weights, window, preferred_element_type=jnp.float32)
        for i, head in enumerate(heads):
            rows = slice(i * count, (i + 1) * count)
            here = lane == sum_column(head) % 128
            at = (sum_column(head) - start) // 128 * 128
            tops = jnp.where(here, top[rows], tops)
            sums = jnp.where(here, mixed[rows, at : at + 128], sums)
            for tile in range(head * DIM // 128, -(-(head + 1) * DIM // 128)):
                part = mixed[rows, tile * 128 - start : (tile + 1) * 128 - start]
                if tile in tiles:
                    inside = (lane >= head * DIM - tile * 128) & (lane < (head + 1) * DIM - tile * 128)
                    part = jnp.where(inside, part, tiles[tile])
                tiles[tile] = part
    return jnp.concatenate([tiles[t] for t in range(WIDTH // 128)], axis=1), tops, sums


def head_columns():
    lane = lax.broadcasted_iota(jnp.int32, (256, WIDTH), 0) % 128
    head = lax.broadcasted_iota(jnp.int32, (256, WIDTH), 1) // DIM
    return jnp.where(lane == jnp.where(head < 3, 112 + head, head), 1.0, 0.0).astype(jnp.bfloat16)


def to_columns(factors, columns):
    high = factors.astype(jnp.bfloat16)
    low = (factors - high.astype(jnp.float32)).astype(jnp.bfloat16)
    return project(jnp.concatenate([high, low], axis=1), columns)


def project(rows, matrix):
    return jnp.dot(rows, matrix, preferred_element_type=jnp.float32)


def kernel(
    lat_hbm, ref_hbm, wq, wk, wv, wo, tq, tk, tv, to, pe_hbm,
    out_s, out_v,
    lat, ref_raw, ref_all, w, pe, queries, mixed_own, top_own, sum_own, columns, flat, own, got, back,
    load_sem, ref_send, ref_recv, go_send, go_recv, back_send, back_recv, out_sem, row_sem, column_sem,
):
    mine_f, mine_r = lax.axis_index("frame"), lax.axis_index("ref")
    zh, y = mine_f // 4, mine_f % 4
    place_r, core = mine_r // 2, mine_r % 2
    zl, x = place_r // 4, place_r % 4

    def frame_at(offset):
        return ((zh + offset[0]) % 4) * 4 + (y + offset[1]) % 4

    def place_at(offset):
        return ((zl + offset[0]) % 2) * 4 + (x + offset[1]) % 4

    loads = [
        pltpu.make_async_copy(ref_hbm, ref_raw, load_sem.at[0]),
        pltpu.make_async_copy(lat_hbm, lat, load_sem.at[1]),
        pltpu.make_async_copy(pe_hbm, pe, load_sem.at[2]),
    ]
    weights = [
        pltpu.make_async_copy(matrix, w.at[i], load_sem.at[3 + i])
        for i, matrix in enumerate((wq, wk, wv, wo, tq, tk, tv, to))
    ]
    loads[0].start()
    barrier = pltpu.get_barrier_semaphore()
    sibling = (mine_f, place_r * 2 + 1 - core)
    greeted = [(mine_f, place_at(offset) * 2 + core) for offset in REF_PEERS]
    greeted += [sibling] + [(frame_at(offset), mine_r) for offset in NEAR]
    for device in greeted:
        pl.semaphore_signal(barrier, inc=1, device_id=device, device_id_type=MESH)
    loads[1].start()
    for copy in weights:
        copy.start()
    loads[2].start()

    loads[0].wait()
    slot = pl.ds(pl.multiple_of((core * 8 + place_r) * PIECES, PIECES), PIECES)
    ref_all[slot, :] = layer_norm(ref_raw[...].astype(jnp.float32)).astype(jnp.bfloat16)
    pl.semaphore_wait(barrier, len(greeted))
    for offset in REF_PEERS:
        copy = pltpu.make_async_remote_copy(
            src_ref=ref_all.at[slot, :], dst_ref=ref_all.at[slot, :],
            send_sem=ref_send.at[0], recv_sem=ref_recv.at[0],
            device_id=(mine_f, place_at(offset) * 2 + core), device_id_type=MESH,
        )
        copy.start()
    for offset in COLUMN_PEERS:
        pl.semaphore_signal(column_sem, inc=1, device_id=(frame_at(offset), mine_r), device_id_type=MESH)

    loads[1].wait()
    normed = layer_norm(lat[...].astype(jnp.float32)).astype(jnp.bfloat16)
    weights[0].wait()
    queries[...] = project(normed, w[0]).astype(jnp.bfloat16)
    weights[1].wait()
    own_keys = project(normed, w[1]).astype(jnp.bfloat16)
    weights[2].wait()
    own_values = project(normed, w[2]).astype(jnp.bfloat16)

    mixed_own[...], top_own[...], sum_own[...] = attend(queries[...], own_keys, own_values)
    columns[...] = head_columns()

    pl.semaphore_wait(column_sem, len(COLUMN_PEERS))
    for offset in ROW_PEERS:
        pl.semaphore_signal(row_sem, inc=1, device_id=(frame_at(offset), mine_r), device_id_type=MESH)

    first = pl.ds(0, len(REF_PEERS) * PIECES)
    from_peers = pltpu.make_async_remote_copy(
        src_ref=ref_all.at[first, :], dst_ref=ref_all.at[first, :],
        send_sem=ref_send.at[0], recv_sem=ref_recv.at[0], device_id=sibling, device_id_type=MESH,
    )
    from_peers.wait_recv()
    half = pl.ds(pl.multiple_of(core * HALF, HALF), HALF)
    to_sibling = pltpu.make_async_remote_copy(
        src_ref=ref_all.at[half, :], dst_ref=ref_all.at[half, :],
        send_sem=ref_send.at[1], recv_sem=ref_recv.at[1], device_id=sibling, device_id_type=MESH,
    )
    to_sibling.start()
    weights[3].wait()
    to_sibling.wait_recv()
    reference = ref_all[...]
    ref_keys = project(reference, w[1]).astype(jnp.bfloat16)
    ref_values = project(reference, w[2]).astype(jnp.bfloat16)

    mixed, top_ref, sum_ref = attend(queries[...], ref_keys, ref_values)
    top = jnp.maximum(top_own[...], top_ref)
    kept_own, kept_ref = jnp.exp2((top_own[...] - top) * FACTOR), jnp.exp2((top_ref - top) * FACTOR)
    scale = 1.0 / (sum_own[...] * kept_own + sum_ref * kept_ref)
    attended = mixed_own[...] * to_columns(kept_own * scale, columns[...])
    attended = (attended + mixed * to_columns(kept_ref * scale, columns[...])).astype(jnp.bfloat16)
    result = lat[...].astype(jnp.float32) + project(attended, w[3])
    own[...] = result.reshape(CHUNKS, FRAMES, EACH, WIDTH).astype(jnp.bfloat16)

    pl.semaphore_wait(row_sem, len(ROW_PEERS))
    for chunk in range(CHUNKS):
        for offset in FRAME_PEERS:
            target = frame_at(offset)
            pltpu.make_async_remote_copy(
                src_ref=own.at[chunk, target], dst_ref=got.at[chunk, mine_f],
                send_sem=go_send.at[chunk], recv_sem=go_recv.at[chunk],
                device_id=(target, mine_r), device_id_type=MESH,
            ).start()
    out_copies = []
    for chunk in range(CHUNKS):
        got[chunk, pl.ds(mine_f, 1)] = own[chunk, pl.ds(mine_f, 1)]
    flat[...] = result.astype(jnp.bfloat16)
    copy = pltpu.make_async_copy(flat, out_s, out_sem.at[CHUNKS])
    copy.start()
    out_copies.append(copy)

    loads[2].wait()
    for copy in weights[4:]:
        copy.wait()
    from_peers.wait_send()
    to_sibling.wait_send()
    row = lax.broadcasted_iota(jnp.int32, (ROWS, ROWS), 0)
    column = lax.broadcasted_iota(jnp.int32, (ROWS, ROWS), 1)
    allowed = row % EACH == column % EACH
    others = pl.ds(0, len(FRAME_PEERS))
    for chunk in range(CHUNKS):
        whole = pltpu.make_async_remote_copy(
            src_ref=own.at[chunk, others], dst_ref=got.at[chunk, others],
            send_sem=go_send.at[chunk], recv_sem=go_recv.at[chunk], device_id=sibling, device_id_type=MESH,
        )
        whole.wait_recv()
        clip = got[chunk].astype(jnp.float32).reshape(ROWS, WIDTH)
        normed = (layer_norm(clip) + pe[...]).astype(jnp.bfloat16)
        time_queries = project(normed, w[4]).astype(jnp.bfloat16)
        time_keys = project(normed, w[5]).astype(jnp.bfloat16)
        time_values = project(normed, w[6]).astype(jnp.bfloat16)
        mixed, _, total = attend(time_queries, time_keys, time_values, allowed)
        attended = (mixed * to_columns(1.0 / total, columns[...])).astype(jnp.bfloat16)
        result = clip + project(attended, w[7])
        back[chunk] = result.reshape(FRAMES, EACH, WIDTH).astype(jnp.bfloat16)
        for offset in FRAME_PEERS:
            target = frame_at(offset)
            pltpu.make_async_remote_copy(
                src_ref=back.at[chunk, target], dst_ref=out_v.at[chunk * FRAMES + mine_f],
                send_sem=back_send.at[chunk], recv_sem=back_recv.at[chunk],
                device_id=(target, mine_r), device_id_type=MESH,
            ).start()
        copy = pltpu.make_async_copy(
            back.at[chunk, mine_f], out_v.at[chunk * FRAMES + mine_f], out_sem.at[chunk]
        )
        copy.start()
        out_copies.append(copy)
        whole.wait_send()

    for copy in out_copies:
        copy.wait()
    for chunk in range(CHUNKS):
        whole = pltpu.make_async_remote_copy(
            src_ref=back.at[chunk, others], dst_ref=out_v.at[pl.ds(chunk * FRAMES, len(FRAME_PEERS))],
            send_sem=back_send.at[chunk], recv_sem=back_recv.at[chunk], device_id=sibling, device_id_type=MESH,
        )
        whole.wait_send()
        whole.wait_recv()


def hand_over(spatial, video, out_s, out_v, held, sem):
    copies = [pltpu.make_async_copy(spatial, out_s, sem.at[0]), pltpu.make_async_copy(held, out_v, sem.at[1])]
    copies[0].start()
    held[...] = video[...].astype(jnp.float32).reshape(TOKENS, WIDTH).astype(jnp.bfloat16)
    copies[1].start()
    for copy in copies:
        copy.wait()


def body(latents, ref_hidden, *matrices):
    any_space = pl.BlockSpec(memory_space=pl.ANY)
    pe = jnp.asarray(np.repeat(sinusoid(FRAMES, WIDTH), EACH, axis=0))
    shape = jax.ShapeDtypeStruct((TOKENS, WIDTH), jnp.bfloat16)
    pieces = jax.ShapeDtypeStruct((CHUNKS * FRAMES, EACH, WIDTH), jnp.bfloat16)
    operands = (latents.reshape(TOKENS, WIDTH), ref_hidden, *matrices, pe)
    spatial, video = pl.pallas_call(
        kernel,
        out_shape=(shape, pieces),
        in_specs=[any_space] * 11,
        out_specs=(any_space, any_space),
        scratch_shapes=[
            pltpu.VMEM((TOKENS, WIDTH), jnp.bfloat16),
            pltpu.VMEM((PIECES, WIDTH), jnp.bfloat16),
            pltpu.VMEM((TOKENS, WIDTH), jnp.bfloat16),
            pltpu.VMEM((8, WIDTH, WIDTH), jnp.bfloat16),
            pltpu.VMEM((ROWS, WIDTH), jnp.float32),
            pltpu.VMEM((TOKENS, WIDTH), jnp.bfloat16),
            pltpu.VMEM((TOKENS, WIDTH), jnp.float32),
            pltpu.VMEM((TOKENS, 128), jnp.float32),
            pltpu.VMEM((TOKENS, 128), jnp.float32),
            pltpu.VMEM((256, WIDTH), jnp.bfloat16),
            pltpu.VMEM((TOKENS, WIDTH), jnp.bfloat16),
            pltpu.VMEM((CHUNKS, FRAMES, EACH, WIDTH), jnp.bfloat16),
            pltpu.VMEM((CHUNKS, FRAMES, EACH, WIDTH), jnp.bfloat16),
            pltpu.VMEM((CHUNKS, FRAMES, EACH, WIDTH), jnp.bfloat16),
            pltpu.SemaphoreType.DMA((11,)),
            pltpu.SemaphoreType.DMA((2,)),
            pltpu.SemaphoreType.DMA((2,)),
            pltpu.SemaphoreType.DMA((CHUNKS,)),
            pltpu.SemaphoreType.DMA((CHUNKS,)),
            pltpu.SemaphoreType.DMA((CHUNKS,)),
            pltpu.SemaphoreType.DMA((CHUNKS,)),
            pltpu.SemaphoreType.DMA((CHUNKS + 1,)),
            pltpu.SemaphoreType.REGULAR,
            pltpu.SemaphoreType.REGULAR,
        ],
        compiler_params=pltpu.CompilerParams(
            collective_id=0, has_side_effects=True, vmem_limit_bytes=48 * 2**20
        ),
        cost_estimate=pl.CostEstimate(flops=3_500_000_000, bytes_accessed=8_000_000, transcendentals=1_500_000),
    )(*[pltpu.with_memory_space_constraint(a, pltpu.HBM) for a in operands])
    spatial, video = pl.pallas_call(
        hand_over,
        out_shape=(shape, shape),
        in_specs=[any_space, pl.BlockSpec(memory_space=pltpu.VMEM)],
        out_specs=(any_space, any_space),
        scratch_shapes=[pltpu.VMEM((TOKENS, WIDTH), jnp.bfloat16), pltpu.SemaphoreType.DMA((2,))],
        compiler_params=pltpu.CompilerParams(vmem_limit_bytes=48 * 2**20),
    )(spatial, video)
    whole = (1, 1, TOKENS, WIDTH)
    return spatial.reshape(whole), video.reshape(whole)


def solution(mesh):
    split = P("ref", "frame", None, None)
    return jax.shard_map(
        body,
        mesh=mesh,
        in_specs=(split, P("ref", None)) + (P(),) * 8,
        out_specs=(split, split),
        check_vma=False,
    )
```

```python
import functools
import math

import jax
import jax.numpy as jnp
import numpy as np
from jax import lax
from jax.experimental import pallas as pl
from jax.experimental.pallas import tpu as pltpu
from jax.sharding import PartitionSpec as P

MESH = pl.DeviceIdType.MESH
HEADS = 8
DIM = 80
WIDTH = 640
TOKENS = 256
FRAMES = 16
PIECES = 16
CHUNKS = 2
ROWS = TOKENS // CHUNKS
EACH = ROWS // FRAMES
EPSILON = 1e-05
SCALE = 1.0 / math.sqrt(DIM)
FACTOR = SCALE * math.log2(math.e)

FRAME_PEERS = sorted(
    [(a, b) for a in range(4) for b in range(4) if a or b],
    key=lambda o: -(2 * min(o[0], 4 - o[0]) + min(o[1], 4 - o[1])),
)
REF_PEERS = sorted([(a, b) for a in range(2) for b in range(4) if a or b], key=lambda o: -(o[0] + min(o[1], 4 - o[1])))
NEAR = [(0, 1), (0, 2), (0, 3), (1, 0), (3, 0)]
ROW_PEERS = [(0, 1), (0, 2), (0, 3)]
COLUMN_PEERS = [(1, 0), (3, 0)]
HALF = TOKENS // 2


def sinusoid(count, width):
    position = np.arange(count, dtype=np.float64)[:, None]
    pair = np.arange(width // 2, dtype=np.float64)[None, :]
    angle = position * np.exp(pair * (-2.0 * math.log(10000.0) / width))
    return np.stack([np.sin(angle), np.cos(angle)], axis=-1).reshape(count, width).astype(np.float32)


def layer_norm(rows):
    center = rows - jnp.mean(rows, axis=-1, keepdims=True)
    spread = jnp.mean(center * center, axis=-1, keepdims=True)
    return center * lax.rsqrt(spread + EPSILON)


GROUPS = (((0, 1, 2), 0), ((3,), 128), ((4,), 256), ((5, 6, 7), 384))


def sum_column(head):
    return 240 + head if head < 3 else {3: 128, 4: 256}.get(head, 384) + head


def attend(queries, keys, values, allowed=None):
    count = queries.shape[0]
    lane = lax.broadcasted_iota(jnp.int32, (1, 128), 1)
    column = lax.broadcasted_iota(jnp.int32, (1, 256), 1)
    tops, sums = jnp.zeros((count, 128), jnp.float32), jnp.ones((count, 128), jnp.float32)
    tiles = {}
    for heads, start in GROUPS:
        cut = slice(start, start + 256)
        stack = []
        for head in heads:
            inside = (column >= head * DIM - start) & (column < (head + 1) * DIM - start)
            stack.append(jnp.where(inside, queries[:, cut], 0.0).astype(jnp.bfloat16))
        scores = lax.dot_general(
            jnp.concatenate(stack, axis=0), keys[:, cut], (((1,), (1,)), ((), ())), preferred_element_type=jnp.float32
        )
        if allowed is not None:
            scores = jnp.where(jnp.concatenate([allowed] * len(heads), axis=0), scores, -1e30)
        top = jnp.max(scores, axis=-1, keepdims=True)
        weights = jnp.exp2((scores - top) * FACTOR).astype(jnp.bfloat16)
        window = values[:, cut]
        for head in heads:
            window = jnp.where(column == sum_column(head) - start, 1.0, window).astype(jnp.bfloat16)
        mixed = jnp.dot(weights, window, preferred_element_type=jnp.float32)
        for i, head in enumerate(heads):
            rows = slice(i * count, (i + 1) * count)
            here = lane == sum_column(head) % 128
            at = (sum_column(head) - start) // 128 * 128
            tops = jnp.where(here, top[rows], tops)
            sums = jnp.where(here, mixed[rows, at : at + 128], sums)
            for tile in range(head * DIM // 128, -(-(head + 1) * DIM // 128)):
                part = mixed[rows, tile * 128 - start : (tile + 1) * 128 - start]
                if tile in tiles:
                    inside = (lane >= head * DIM - tile * 128) & (lane < (head + 1) * DIM - tile * 128)
                    part = jnp.where(inside, part, tiles[tile])
                tiles[tile] = part
    return jnp.concatenate([tiles[t] for t in range(WIDTH // 128)], axis=1), tops, sums


def head_columns():
    lane = lax.broadcasted_iota(jnp.int32, (256, WIDTH), 0) % 128
    head = lax.broadcasted_iota(jnp.int32, (256, WIDTH), 1) // DIM
    return jnp.where(lane == jnp.where(head < 3, 112 + head, head), 1.0, 0.0).astype(jnp.bfloat16)


def to_columns(factors, columns):
    high = factors.astype(jnp.bfloat16)
    low = (factors - high.astype(jnp.float32)).astype(jnp.bfloat16)
    return project(jnp.concatenate([high, low], axis=1), columns)


def project(rows, matrix):
    return jnp.dot(rows, matrix, preferred_element_type=jnp.float32)


def kernel(
    lat_hbm, ref_hbm, wq, wk, wv, wo, tq, tk, tv, to, pe_hbm,
    out_s, out_v,
    lat, ref_raw, ref_all, w, pe, queries, mixed_own, top_own, sum_own, columns, flat, own, got, back,
    load_sem, ref_send, ref_recv, go_send, go_recv, back_send, back_recv, out_sem, row_sem, column_sem,
):
    mine_f, mine_r = lax.axis_index("frame"), lax.axis_index("ref")
    zh, y = mine_f // 4, mine_f % 4
    place_r, core = mine_r // 2, mine_r % 2
    zl, x = place_r // 4, place_r % 4

    def frame_at(offset):
        return ((zh + offset[0]) % 4) * 4 + (y + offset[1]) % 4

    def place_at(offset):
        return ((zl + offset[0]) % 2) * 4 + (x + offset[1]) % 4

    loads = [
        pltpu.make_async_copy(ref_hbm, ref_raw, load_sem.at[0]),
        pltpu.make_async_copy(lat_hbm, lat, load_sem.at[1]),
        pltpu.make_async_copy(pe_hbm, pe, load_sem.at[2]),
    ]
    weights = [
        pltpu.make_async_copy(matrix, w.at[i], load_sem.at[3 + i])
        for i, matrix in enumerate((wq, wk, wv, wo, tq, tk, tv, to))
    ]
    loads[0].start()
    barrier = pltpu.get_barrier_semaphore()
    sibling = (mine_f, place_r * 2 + 1 - core)
    greeted = [(mine_f, place_at(offset) * 2 + core) for offset in REF_PEERS]
    greeted += [sibling] + [(frame_at(offset), mine_r) for offset in NEAR]
    for device in greeted:
        pl.semaphore_signal(barrier, inc=1, device_id=device, device_id_type=MESH)
    loads[1].start()
    for copy in weights:
        copy.start()
    loads[2].start()

    loads[0].wait()
    slot = pl.ds(pl.multiple_of((core * 8 + place_r) * PIECES, PIECES), PIECES)
    ref_all[slot, :] = layer_norm(ref_raw[...].astype(jnp.float32)).astype(jnp.bfloat16)
    pl.semaphore_wait(barrier, len(greeted))
    for offset in REF_PEERS:
        copy = pltpu.make_async_remote_copy(
            src_ref=ref_all.at[slot, :], dst_ref=ref_all.at[slot, :],
            send_sem=ref_send.at[0], recv_sem=ref_recv.at[0],
            device_id=(mine_f, place_at(offset) * 2 + core), device_id_type=MESH,
        )
        copy.start()
    for offset in COLUMN_PEERS:
        pl.semaphore_signal(column_sem, inc=1, device_id=(frame_at(offset), mine_r), device_id_type=MESH)

    loads[1].wait()
    normed = layer_norm(lat[...].astype(jnp.float32)).astype(jnp.bfloat16)
    weights[0].wait()
    queries[...] = project(normed, w[0]).astype(jnp.bfloat16)
    weights[1].wait()
    own_keys = project(normed, w[1]).astype(jnp.bfloat16)
    weights[2].wait()
    own_values = project(normed, w[2]).astype(jnp.bfloat16)

    mixed_own[...], top_own[...], sum_own[...] = attend(queries[...], own_keys, own_values)
    columns[...] = head_columns()

    pl.semaphore_wait(column_sem, len(COLUMN_PEERS))
    for offset in ROW_PEERS:
        pl.semaphore_signal(row_sem, inc=1, device_id=(frame_at(offset), mine_r), device_id_type=MESH)

    first = pl.ds(0, len(REF_PEERS) * PIECES)
    from_peers = pltpu.make_async_remote_copy(
        src_ref=ref_all.at[first, :], dst_ref=ref_all.at[first, :],
        send_sem=ref_send.at[0], recv_sem=ref_recv.at[0], device_id=sibling, device_id_type=MESH,
    )
    from_peers.wait_recv()
    half = pl.ds(pl.multiple_of(core * HALF, HALF), HALF)
    to_sibling = pltpu.make_async_remote_copy(
        src_ref=ref_all.at[half, :], dst_ref=ref_all.at[half, :],
        send_sem=ref_send.at[1], recv_sem=ref_recv.at[1], device_id=sibling, device_id_type=MESH,
    )
    to_sibling.start()
    weights[3].wait()
    to_sibling.wait_recv()
    reference = ref_all[...]
    ref_keys = project(reference, w[1]).astype(jnp.bfloat16)
    ref_values = project(reference, w[2]).astype(jnp.bfloat16)

    for part in range(2):
        rows = slice(part * HALF, (part + 1) * HALF)
        mixed, top_ref, sum_ref = attend(queries[rows, :], ref_keys, ref_values)
        top = jnp.maximum(top_own[rows, :], top_ref)
        kept_own, kept_ref = jnp.exp2((top_own[rows, :] - top) * FACTOR), jnp.exp2((top_ref - top) * FACTOR)
        scale = 1.0 / (sum_own[rows, :] * kept_own + sum_ref * kept_ref)
        attended = mixed_own[rows, :] * to_columns(kept_own * scale, columns[...])
        attended = (attended + mixed * to_columns(kept_ref * scale, columns[...])).astype(jnp.bfloat16)
        result = lat[rows, :].astype(jnp.float32) + project(attended, w[3])
        chunks = slice(part * CHUNKS // 2, (part + 1) * CHUNKS // 2)
        own[chunks] = result.reshape(CHUNKS // 2, FRAMES, EACH, WIDTH).astype(jnp.bfloat16)
        flat[rows, :] = result.astype(jnp.bfloat16)
        if part == 0:
            pl.semaphore_wait(row_sem, len(ROW_PEERS))
        for chunk in range(CHUNKS)[chunks]:
            for offset in FRAME_PEERS:
                target = frame_at(offset)
                pltpu.make_async_remote_copy(
                    src_ref=own.at[chunk, target], dst_ref=got.at[chunk, mine_f],
                    send_sem=go_send.at[chunk], recv_sem=go_recv.at[chunk],
                    device_id=(target, mine_r), device_id_type=MESH,
                ).start()
    out_copies = []
    for chunk in range(CHUNKS):
        got[chunk, pl.ds(mine_f, 1)] = own[chunk, pl.ds(mine_f, 1)]
    copy = pltpu.make_async_copy(flat, out_s, out_sem.at[CHUNKS])
    copy.start()
    out_copies.append(copy)

    loads[2].wait()
    for copy in weights[4:]:
        copy.wait()
    from_peers.wait_send()
    to_sibling.wait_send()
    row = lax.broadcasted_iota(jnp.int32, (ROWS, ROWS), 0)
    column = lax.broadcasted_iota(jnp.int32, (ROWS, ROWS), 1)
    allowed = row % EACH == column % EACH
    others = pl.ds(0, len(FRAME_PEERS))
    for chunk in range(CHUNKS):
        whole = pltpu.make_async_remote_copy(
            src_ref=own.at[chunk, others], dst_ref=got.at[chunk, others],
            send_sem=go_send.at[chunk], recv_sem=go_recv.at[chunk], device_id=sibling, device_id_type=MESH,
        )
        whole.wait_recv()
        clip = got[chunk].astype(jnp.float32).reshape(ROWS, WIDTH)
        normed = (layer_norm(clip) + pe[...]).astype(jnp.bfloat16)
        time_queries = project(normed, w[4]).astype(jnp.bfloat16)
        time_keys = project(normed, w[5]).astype(jnp.bfloat16)
        time_values = project(normed, w[6]).astype(jnp.bfloat16)
        mixed, _, total = attend(time_queries, time_keys, time_values, allowed)
        attended = (mixed * to_columns(1.0 / total, columns[...])).astype(jnp.bfloat16)
        result = clip + project(attended, w[7])
        back[chunk] = result.reshape(FRAMES, EACH, WIDTH).astype(jnp.bfloat16)
        def send_back(target, chunk=chunk):
            pltpu.make_async_remote_copy(
                src_ref=back.at[chunk, target], dst_ref=out_v.at[chunk * FRAMES + mine_f],
                send_sem=back_send.at[chunk], recv_sem=back_recv.at[chunk],
                device_id=(target, mine_r), device_id_type=MESH,
            ).start()

        pl.loop(0, mine_f)(send_back)
        pl.loop(mine_f + 1, FRAMES)(send_back)
        copy = pltpu.make_async_copy(
            back.at[chunk, mine_f], out_v.at[chunk * FRAMES + mine_f], out_sem.at[chunk]
        )
        copy.start()
        out_copies.append(copy)
        whole.wait_send()

    for copy in out_copies:
        copy.wait()
    for chunk in range(CHUNKS):
        whole = pltpu.make_async_remote_copy(
            src_ref=back.at[chunk, others], dst_ref=out_v.at[pl.ds(chunk * FRAMES, len(FRAME_PEERS))],
            send_sem=back_send.at[chunk], recv_sem=back_recv.at[chunk], device_id=sibling, device_id_type=MESH,
        )
        whole.wait_send()
        whole.wait_recv()


def hand_over(spatial, video, out_s, out_v, held, sem):
    copies = [pltpu.make_async_copy(spatial, out_s, sem.at[0]), pltpu.make_async_copy(held, out_v, sem.at[1])]
    copies[0].start()
    held[...] = video[...].astype(jnp.float32).reshape(TOKENS, WIDTH).astype(jnp.bfloat16)
    copies[1].start()
    for copy in copies:
        copy.wait()


def body(latents, ref_hidden, *matrices):
    any_space = pl.BlockSpec(memory_space=pl.ANY)
    pe = jnp.asarray(np.repeat(sinusoid(FRAMES, WIDTH), EACH, axis=0))
    shape = jax.ShapeDtypeStruct((TOKENS, WIDTH), jnp.bfloat16)
    pieces = jax.ShapeDtypeStruct((CHUNKS * FRAMES, EACH, WIDTH), jnp.bfloat16)
    operands = (latents.reshape(TOKENS, WIDTH), ref_hidden, *matrices, pe)
    spatial, video = pl.pallas_call(
        kernel,
        out_shape=(shape, pieces),
        in_specs=[any_space] * 11,
        out_specs=(any_space, any_space),
        scratch_shapes=[
            pltpu.VMEM((TOKENS, WIDTH), jnp.bfloat16),
            pltpu.VMEM((PIECES, WIDTH), jnp.bfloat16),
            pltpu.VMEM((TOKENS, WIDTH), jnp.bfloat16),
            pltpu.VMEM((8, WIDTH, WIDTH), jnp.bfloat16),
            pltpu.VMEM((ROWS, WIDTH), jnp.float32),
            pltpu.VMEM((TOKENS, WIDTH), jnp.bfloat16),
            pltpu.VMEM((TOKENS, WIDTH), jnp.float32),
            pltpu.VMEM((TOKENS, 128), jnp.float32),
            pltpu.VMEM((TOKENS, 128), jnp.float32),
            pltpu.VMEM((256, WIDTH), jnp.bfloat16),
            pltpu.VMEM((TOKENS, WIDTH), jnp.bfloat16),
            pltpu.VMEM((CHUNKS, FRAMES, EACH, WIDTH), jnp.bfloat16),
            pltpu.VMEM((CHUNKS, FRAMES, EACH, WIDTH), jnp.bfloat16),
            pltpu.VMEM((CHUNKS, FRAMES, EACH, WIDTH), jnp.bfloat16),
            pltpu.SemaphoreType.DMA((11,)),
            pltpu.SemaphoreType.DMA((2,)),
            pltpu.SemaphoreType.DMA((2,)),
            pltpu.SemaphoreType.DMA((CHUNKS,)),
            pltpu.SemaphoreType.DMA((CHUNKS,)),
            pltpu.SemaphoreType.DMA((CHUNKS,)),
            pltpu.SemaphoreType.DMA((CHUNKS,)),
            pltpu.SemaphoreType.DMA((CHUNKS + 1,)),
            pltpu.SemaphoreType.REGULAR,
            pltpu.SemaphoreType.REGULAR,
        ],
        compiler_params=pltpu.CompilerParams(
            collective_id=0, has_side_effects=True, vmem_limit_bytes=48 * 2**20
        ),
        cost_estimate=pl.CostEstimate(flops=3_500_000_000, bytes_accessed=8_000_000, transcendentals=1_500_000),
    )(*[pltpu.with_memory_space_constraint(a, pltpu.HBM) for a in operands])
    spatial, video = pl.pallas_call(
        hand_over,
        out_shape=(shape, shape),
        in_specs=[any_space, pl.BlockSpec(memory_space=pltpu.VMEM)],
        out_specs=(any_space, any_space),
        scratch_shapes=[pltpu.VMEM((TOKENS, WIDTH), jnp.bfloat16), pltpu.SemaphoreType.DMA((2,))],
        compiler_params=pltpu.CompilerParams(vmem_limit_bytes=48 * 2**20),
    )(spatial, video)
    whole = (1, 1, TOKENS, WIDTH)
    return spatial.reshape(whole), video.reshape(whole)


def solution(mesh):
    split = P("ref", "frame", None, None)
    return jax.shard_map(
        body,
        mesh=mesh,
        in_specs=(split, P("ref", None)) + (P(),) * 8,
        out_specs=(split, split),
        check_vma=False,
    )
```

```python
import functools
import math

import jax
import jax.numpy as jnp
import numpy as np
from jax import lax
from jax.experimental import pallas as pl
from jax.experimental.pallas import tpu as pltpu
from jax.sharding import PartitionSpec as P

MESH = pl.DeviceIdType.MESH
HEADS = 8
DIM = 80
WIDTH = 640
TOKENS = 256
FRAMES = 16
PIECES = 16
CHUNKS = 2
ROWS = TOKENS // CHUNKS
EACH = ROWS // FRAMES
EPSILON = 1e-05
SCALE = 1.0 / math.sqrt(DIM)
FACTOR = SCALE * math.log2(math.e)

FRAME_PEERS = sorted(
    [(a, b) for a in range(4) for b in range(4) if a or b],
    key=lambda o: -(2 * min(o[0], 4 - o[0]) + min(o[1], 4 - o[1])),
)
REF_PEERS = sorted([(a, b) for a in range(2) for b in range(4) if a or b], key=lambda o: -(o[0] + min(o[1], 4 - o[1])))
NEAR = [(0, 1), (0, 2), (0, 3), (1, 0), (3, 0)]
ROW_PEERS = [(0, 1), (0, 2), (0, 3)]
COLUMN_PEERS = [(1, 0), (3, 0)]
HALF = TOKENS // 2


def sinusoid(count, width):
    position = np.arange(count, dtype=np.float64)[:, None]
    pair = np.arange(width // 2, dtype=np.float64)[None, :]
    angle = position * np.exp(pair * (-2.0 * math.log(10000.0) / width))
    return np.stack([np.sin(angle), np.cos(angle)], axis=-1).reshape(count, width).astype(np.float32)


def layer_norm(rows):
    center = rows - jnp.mean(rows, axis=-1, keepdims=True)
    spread = jnp.mean(center * center, axis=-1, keepdims=True)
    return center * lax.rsqrt(spread + EPSILON)


GROUPS = (((0, 1, 2), 0), ((3,), 128), ((4,), 256), ((5, 6, 7), 384))


def sum_column(head):
    return 240 + head if head < 3 else {3: 128, 4: 256}.get(head, 384) + head


def attend(queries, keys, values, allowed=None):
    count = queries.shape[0]
    lane = lax.broadcasted_iota(jnp.int32, (1, 128), 1)
    column = lax.broadcasted_iota(jnp.int32, (1, 256), 1)
    tops, sums = jnp.zeros((count, 128), jnp.float32), jnp.ones((count, 128), jnp.float32)
    tiles = {}
    for heads, start in GROUPS:
        cut = slice(start, start + 256)
        stack = []
        for head in heads:
            inside = (column >= head * DIM - start) & (column < (head + 1) * DIM - start)
            stack.append(jnp.where(inside, queries[:, cut], 0.0).astype(jnp.bfloat16))
        scores = lax.dot_general(
            jnp.concatenate(stack, axis=0), keys[:, cut], (((1,), (1,)), ((), ())), preferred_element_type=jnp.float32
        )
        if allowed is not None:
            scores = jnp.where(jnp.concatenate([allowed] * len(heads), axis=0), scores, -1e30)
        top = jnp.max(scores, axis=-1, keepdims=True)
        weights = jnp.exp2((scores - top) * FACTOR).astype(jnp.bfloat16)
        window = values[:, cut]
        for head in heads:
            window = jnp.where(column == sum_column(head) - start, 1.0, window).astype(jnp.bfloat16)
        mixed = jnp.dot(weights, window, preferred_element_type=jnp.float32)
        for i, head in enumerate(heads):
            rows = slice(i * count, (i + 1) * count)
            here = lane == sum_column(head) % 128
            at = (sum_column(head) - start) // 128 * 128
            tops = jnp.where(here, top[rows], tops)
            sums = jnp.where(here, mixed[rows, at : at + 128], sums)
            for tile in range(head * DIM // 128, -(-(head + 1) * DIM // 128)):
                part = mixed[rows, tile * 128 - start : (tile + 1) * 128 - start]
                if tile in tiles:
                    inside = (lane >= head * DIM - tile * 128) & (lane < (head + 1) * DIM - tile * 128)
                    part = jnp.where(inside, part, tiles[tile])
                tiles[tile] = part
    return jnp.concatenate([tiles[t] for t in range(WIDTH // 128)], axis=1), tops, sums


def head_columns():
    lane = lax.broadcasted_iota(jnp.int32, (256, WIDTH), 0) % 128
    head = lax.broadcasted_iota(jnp.int32, (256, WIDTH), 1) // DIM
    return jnp.where(lane == jnp.where(head < 3, 112 + head, head), 1.0, 0.0).astype(jnp.bfloat16)


def to_columns(factors, columns):
    high = factors.astype(jnp.bfloat16)
    low = (factors - high.astype(jnp.float32)).astype(jnp.bfloat16)
    return project(jnp.concatenate([high, low], axis=1), columns)


def project(rows, matrix):
    return jnp.dot(rows, matrix, preferred_element_type=jnp.float32)


def kernel(
    lat_hbm, ref_hbm, wq, wk, wv, wo, tq, tk, tv, to, pe_hbm,
    out_s, out_v,
    lat, ref_raw, ref_all, w, pe, queries, mixed_own, top_own, sum_own, columns, flat, own, got, back,
    load_sem, ref_send, ref_recv, go_send, go_recv, back_send, back_recv, out_sem, row_sem, column_sem,
):
    mine_f, mine_r = lax.axis_index("frame"), lax.axis_index("ref")
    zh, y = mine_f // 4, mine_f % 4
    place_r, core = mine_r // 2, mine_r % 2
    zl, x = place_r // 4, place_r % 4

    def frame_at(offset):
        return ((zh + offset[0]) % 4) * 4 + (y + offset[1]) % 4

    def place_at(offset):
        return ((zl + offset[0]) % 2) * 4 + (x + offset[1]) % 4

    loads = [
        pltpu.make_async_copy(ref_hbm, ref_raw, load_sem.at[0]),
        pltpu.make_async_copy(lat_hbm, lat, load_sem.at[1]),
        pltpu.make_async_copy(pe_hbm, pe, load_sem.at[2]),
    ]
    weights = [
        pltpu.make_async_copy(matrix, w.at[:, pl.ds(i * WIDTH, WIDTH)], load_sem.at[3 + i])
        for i, matrix in enumerate((wq, wk, wv, wo, tq, tk, tv, to))
    ]
    loads[0].start()
    barrier = pltpu.get_barrier_semaphore()
    sibling = (mine_f, place_r * 2 + 1 - core)
    greeted = [(mine_f, place_at(offset) * 2 + core) for offset in REF_PEERS]
    greeted += [sibling] + [(frame_at(offset), mine_r) for offset in NEAR]
    for device in greeted:
        pl.semaphore_signal(barrier, inc=1, device_id=device, device_id_type=MESH)
    loads[1].start()
    for copy in weights:
        copy.start()
    loads[2].start()

    loads[0].wait()
    slot = pl.ds(pl.multiple_of((core * 8 + place_r) * PIECES, PIECES), PIECES)
    ref_all[slot, :] = layer_norm(ref_raw[...].astype(jnp.float32)).astype(jnp.bfloat16)
    pl.semaphore_wait(barrier, len(greeted))
    for offset in REF_PEERS:
        copy = pltpu.make_async_remote_copy(
            src_ref=ref_all.at[slot, :], dst_ref=ref_all.at[slot, :],
            send_sem=ref_send.at[0], recv_sem=ref_recv.at[0],
            device_id=(mine_f, place_at(offset) * 2 + core), device_id_type=MESH,
        )
        copy.start()
    for offset in COLUMN_PEERS:
        pl.semaphore_signal(column_sem, inc=1, device_id=(frame_at(offset), mine_r), device_id_type=MESH)

    loads[1].wait()
    normed = layer_norm(lat[...].astype(jnp.float32)).astype(jnp.bfloat16)
    weights[0].wait()
    queries[...] = project(normed, w[:, 0 * WIDTH : 1 * WIDTH]).astype(jnp.bfloat16)
    weights[1].wait()
    own_keys = project(normed, w[:, 1 * WIDTH : 2 * WIDTH]).astype(jnp.bfloat16)
    weights[2].wait()
    own_values = project(normed, w[:, 2 * WIDTH : 3 * WIDTH]).astype(jnp.bfloat16)

    mixed_own[...], top_own[...], sum_own[...] = attend(queries[...], own_keys, own_values)
    columns[...] = head_columns()

    pl.semaphore_wait(column_sem, len(COLUMN_PEERS))
    for offset in ROW_PEERS:
        pl.semaphore_signal(row_sem, inc=1, device_id=(frame_at(offset), mine_r), device_id_type=MESH)

    first = pl.ds(0, len(REF_PEERS) * PIECES)
    from_peers = pltpu.make_async_remote_copy(
        src_ref=ref_all.at[first, :], dst_ref=ref_all.at[first, :],
        send_sem=ref_send.at[0], recv_sem=ref_recv.at[0], device_id=sibling, device_id_type=MESH,
    )
    from_peers.wait_recv()
    half = pl.ds(pl.multiple_of(core * HALF, HALF), HALF)
    to_sibling = pltpu.make_async_remote_copy(
        src_ref=ref_all.at[half, :], dst_ref=ref_all.at[half, :],
        send_sem=ref_send.at[1], recv_sem=ref_recv.at[1], device_id=sibling, device_id_type=MESH,
    )
    to_sibling.start()
    weights[3].wait()
    to_sibling.wait_recv()
    reference = ref_all[...]
    both = project(reference, w[:, WIDTH : 3 * WIDTH]).astype(jnp.bfloat16)
    ref_keys, ref_values = both[:, :WIDTH], both[:, WIDTH:]

    for part in range(2):
        rows = slice(part * HALF, (part + 1) * HALF)
        mixed, top_ref, sum_ref = attend(queries[rows, :], ref_keys, ref_values)
        top = jnp.maximum(top_own[rows, :], top_ref)
        kept_own, kept_ref = jnp.exp2((top_own[rows, :] - top) * FACTOR), jnp.exp2((top_ref - top) * FACTOR)
        scale = 1.0 / (sum_own[rows, :] * kept_own + sum_ref * kept_ref)
        attended = mixed_own[rows, :] * to_columns(kept_own * scale, columns[...])
        attended = (attended + mixed * to_columns(kept_ref * scale, columns[...])).astype(jnp.bfloat16)
        result = lat[rows, :].astype(jnp.float32) + project(attended, w[:, 3 * WIDTH : 4 * WIDTH])
        chunks = slice(part * CHUNKS // 2, (part + 1) * CHUNKS // 2)
        own[chunks] = result.reshape(CHUNKS // 2, FRAMES, EACH, WIDTH).astype(jnp.bfloat16)
        flat[rows, :] = result.astype(jnp.bfloat16)
        if part == 0:
            pl.semaphore_wait(row_sem, len(ROW_PEERS))
        for chunk in range(CHUNKS)[chunks]:
            for offset in FRAME_PEERS:
                target = frame_at(offset)
                pltpu.make_async_remote_copy(
                    src_ref=own.at[chunk, target], dst_ref=got.at[chunk, mine_f],
                    send_sem=go_send.at[chunk], recv_sem=go_recv.at[chunk],
                    device_id=(target, mine_r), device_id_type=MESH,
                ).start()
    out_copies = []
    for chunk in range(CHUNKS):
        got[chunk, pl.ds(mine_f, 1)] = own[chunk, pl.ds(mine_f, 1)]
    copy = pltpu.make_async_copy(flat, out_s, out_sem.at[CHUNKS])
    copy.start()
    out_copies.append(copy)

    loads[2].wait()
    for copy in weights[4:]:
        copy.wait()
    from_peers.wait_send()
    to_sibling.wait_send()
    row = lax.broadcasted_iota(jnp.int32, (ROWS, ROWS), 0)
    column = lax.broadcasted_iota(jnp.int32, (ROWS, ROWS), 1)
    allowed = row % EACH == column % EACH
    others = pl.ds(0, len(FRAME_PEERS))
    for chunk in range(CHUNKS):
        whole = pltpu.make_async_remote_copy(
            src_ref=own.at[chunk, others], dst_ref=got.at[chunk, others],
            send_sem=go_send.at[chunk], recv_sem=go_recv.at[chunk], device_id=sibling, device_id_type=MESH,
        )
        whole.wait_recv()
        clip = got[chunk].astype(jnp.float32).reshape(ROWS, WIDTH)
        normed = (layer_norm(clip) + pe[...]).astype(jnp.bfloat16)
        rows = project(normed, w[:, 4 * WIDTH : 7 * WIDTH]).astype(jnp.bfloat16)
        time_queries, time_keys, time_values = (rows[:, i * WIDTH : (i + 1) * WIDTH] for i in range(3))
        mixed, _, total = attend(time_queries, time_keys, time_values, allowed)
        attended = (mixed * to_columns(1.0 / total, columns[...])).astype(jnp.bfloat16)
        result = clip + project(attended, w[:, 7 * WIDTH : 8 * WIDTH])
        back[chunk] = result.reshape(FRAMES, EACH, WIDTH).astype(jnp.bfloat16)
        def send_back(target, chunk=chunk):
            pltpu.make_async_remote_copy(
                src_ref=back.at[chunk, target], dst_ref=out_v.at[chunk * FRAMES + mine_f],
                send_sem=back_send.at[chunk], recv_sem=back_recv.at[chunk],
                device_id=(target, mine_r), device_id_type=MESH,
            ).start()

        pl.loop(0, mine_f)(send_back)
        pl.loop(mine_f + 1, FRAMES)(send_back)
        copy = pltpu.make_async_copy(
            back.at[chunk, mine_f], out_v.at[chunk * FRAMES + mine_f], out_sem.at[chunk]
        )
        copy.start()
        out_copies.append(copy)
        whole.wait_send()

    for copy in out_copies:
        copy.wait()
    for chunk in range(CHUNKS):
        whole = pltpu.make_async_remote_copy(
            src_ref=back.at[chunk, others], dst_ref=out_v.at[pl.ds(chunk * FRAMES, len(FRAME_PEERS))],
            send_sem=back_send.at[chunk], recv_sem=back_recv.at[chunk], device_id=sibling, device_id_type=MESH,
        )
        whole.wait_send()
        whole.wait_recv()


def hand_over(spatial, video, out_s, out_v, held, sem):
    copies = [pltpu.make_async_copy(spatial, out_s, sem.at[0]), pltpu.make_async_copy(held, out_v, sem.at[1])]
    copies[0].start()
    held[...] = video[...].astype(jnp.float32).reshape(TOKENS, WIDTH).astype(jnp.bfloat16)
    copies[1].start()
    for copy in copies:
        copy.wait()


def body(latents, ref_hidden, *matrices):
    any_space = pl.BlockSpec(memory_space=pl.ANY)
    pe = jnp.asarray(np.repeat(sinusoid(FRAMES, WIDTH), EACH, axis=0))
    shape = jax.ShapeDtypeStruct((TOKENS, WIDTH), jnp.bfloat16)
    pieces = jax.ShapeDtypeStruct((CHUNKS * FRAMES, EACH, WIDTH), jnp.bfloat16)
    operands = (latents.reshape(TOKENS, WIDTH), ref_hidden, *matrices, pe)
    spatial, video = pl.pallas_call(
        kernel,
        out_shape=(shape, pieces),
        in_specs=[any_space] * 11,
        out_specs=(any_space, any_space),
        scratch_shapes=[
            pltpu.VMEM((TOKENS, WIDTH), jnp.bfloat16),
            pltpu.VMEM((PIECES, WIDTH), jnp.bfloat16),
            pltpu.VMEM((TOKENS, WIDTH), jnp.bfloat16),
            pltpu.VMEM((WIDTH, 8 * WIDTH), jnp.bfloat16),
            pltpu.VMEM((ROWS, WIDTH), jnp.float32),
            pltpu.VMEM((TOKENS, WIDTH), jnp.bfloat16),
            pltpu.VMEM((TOKENS, WIDTH), jnp.float32),
            pltpu.VMEM((TOKENS, 128), jnp.float32),
            pltpu.VMEM((TOKENS, 128), jnp.float32),
            pltpu.VMEM((256, WIDTH), jnp.bfloat16),
            pltpu.VMEM((TOKENS, WIDTH), jnp.bfloat16),
            pltpu.VMEM((CHUNKS, FRAMES, EACH, WIDTH), jnp.bfloat16),
            pltpu.VMEM((CHUNKS, FRAMES, EACH, WIDTH), jnp.bfloat16),
            pltpu.VMEM((CHUNKS, FRAMES, EACH, WIDTH), jnp.bfloat16),
            pltpu.SemaphoreType.DMA((11,)),
            pltpu.SemaphoreType.DMA((2,)),
            pltpu.SemaphoreType.DMA((2,)),
            pltpu.SemaphoreType.DMA((CHUNKS,)),
            pltpu.SemaphoreType.DMA((CHUNKS,)),
            pltpu.SemaphoreType.DMA((CHUNKS,)),
            pltpu.SemaphoreType.DMA((CHUNKS,)),
            pltpu.SemaphoreType.DMA((CHUNKS + 1,)),
            pltpu.SemaphoreType.REGULAR,
            pltpu.SemaphoreType.REGULAR,
        ],
        compiler_params=pltpu.CompilerParams(
            collective_id=0, has_side_effects=True, vmem_limit_bytes=48 * 2**20
        ),
        cost_estimate=pl.CostEstimate(flops=3_500_000_000, bytes_accessed=8_000_000, transcendentals=1_500_000),
    )(*[pltpu.with_memory_space_constraint(a, pltpu.HBM) for a in operands])
    spatial, video = pl.pallas_call(
        hand_over,
        out_shape=(shape, shape),
        in_specs=[any_space, pl.BlockSpec(memory_space=pltpu.VMEM)],
        out_specs=(any_space, any_space),
        scratch_shapes=[pltpu.VMEM((TOKENS, WIDTH), jnp.bfloat16), pltpu.SemaphoreType.DMA((2,))],
        compiler_params=pltpu.CompilerParams(vmem_limit_bytes=48 * 2**20),
    )(spatial, video)
    whole = (1, 1, TOKENS, WIDTH)
    return spatial.reshape(whole), video.reshape(whole)


def solution(mesh):
    split = P("ref", "frame", None, None)
    return jax.shard_map(
        body,
        mesh=mesh,
        in_specs=(split, P("ref", None)) + (P(),) * 8,
        out_specs=(split, split),
        check_vma=False,
    )
```
